768 devices in a mesh: expert: 8 (over y_hi, x), edata: 96 (over y_lo, z, core).
Axes of the slice: x: 4, y: 8 (y_hi: 2, y_lo: 4; y = y_hi * 4 + y_lo), z: 12, core: 2. Of those that a mesh axis runs over, the one named last changes fastest.
Arguments:
- grad_out: bfloat16 [196608, 2560], P(('expert', 'edata')), may hold values from -6 to 6
- route_weight: float32 [196608], P(('expert', 'edata')), may hold values from 0.05 to 1
- counts: int32 [6144], P(('expert', 'edata')), may hold values from 1 to 32, as said below
- preact: bfloat16 [196608, 1536], P(('expert', 'edata')), may hold values from -24 to 24
- down_weight: bfloat16 [8, 768, 2560], P('expert'), may hold values from -0.21875 to 0.21875
Outputs:
- grad_preact: bfloat16 [196608, 1536], P(('expert', 'edata'))
- weight_grad: float32 [8, 768, 2560], P('expert', 'edata')
- route_grad: float32 [196608], P(('expert', 'edata'))
The draws below stay inside these ranges and needn't reach their ends.
Inputs may be any that keep to these rules, and one draw needn't show every extreme that they name: `counts`: every count is at most 32; in every draw one expert device receives 32 live rows from every sending device.
All inputs are finite; a program needn't handle non-finite values.
Results may differ from the reference program's by a relative error of at most 0.0085.
Values may be sent and summed in bfloat16 or wider, within the bound.
No kernel may reach another device: no remote copies, remote signals or barrier semaphores. Data moves between devices by JAX's collectives and lax.ppermute only.
A program may use at most 32 MiB of HBM per device.

```python
import math
import jax
import jax.numpy as jnp
from jax import lax

D = 2560
H = 768
CAP = 32
ROWS = 196608
N_EXPERT = 8
N_EDATA = 96


def draw_counts(key, part):
    key = jax.random.fold_in(key, 7)
    first_key, second_key = jax.random.split(key)
    base_counts = jax.random.randint(first_key, (N_EXPERT, N_EDATA, N_EXPERT), 1, CAP + 1)
    full_expert = jax.random.randint(second_key, (), 0, N_EXPERT)
    destination = lax.broadcasted_iota(jnp.int32, (N_EXPERT, N_EDATA, N_EXPERT), 2)
    filled = jnp.where(destination == full_expert, CAP, base_counts)
    return filled.reshape(N_EXPERT * N_EDATA * N_EXPERT).astype(jnp.int32)


def strengthened(values, stream_key, source, target, parts, factor):
    owner, partner = [(jnp.arange(values.shape[axis_at]) // (values.shape[axis_at] // parts)).reshape([-1 if axis == axis_at else 1 for axis in range(values.ndim)]) for axis_at in (source, target)]
    chosen = jax.random.permutation(stream_key, parts)[partner]
    strong = (owner == chosen) | (owner == (partner + parts // 2) % parts)
    return jnp.where(strong, factor * values, values)


def shard_levels(own_key, extent, shards, least, top_value):
    loudness = 1.0
    for axis_at, blocks in shards:
        heights = jax.random.uniform(jax.random.fold_in(jax.random.fold_in(own_key, 6), axis_at), (blocks,), jnp.float32, least / len(shards), top_value / len(shards))
        loudness = loudness * jnp.repeat(jnp.exp(heights), extent[axis_at] // blocks).reshape((-1,) + (1,) * (len(extent) - 1 - axis_at))
    return loudness


def normal_values(stream_key, dims, deviation, most, shards=(), held_as=jnp.bfloat16):
    values = jax.random.normal(stream_key, dims, jnp.float32) * deviation
    if len(shards) > 0:
        values = shard_levels(stream_key, dims, shards, -0.22, 0.18) * values
    return jnp.clip(values, min=-most, max=most).astype(held_as)


def noise_with(stream_key, dims, scale, limit, cuts, heavy, kind=jnp.bfloat16):
    result = scale * jax.random.normal(stream_key, dims, jnp.float32)
    if cuts:
        result = result * shard_levels(stream_key, dims, cuts, -0.22, 0.18)
    return jnp.clip(strengthened(result, jax.random.fold_in(stream_key, 3), *heavy), -limit, limit).astype(kind)


def setup_inputs(seed: int = 0) -> dict:
    seeds = jax.random.split(jax.random.key(seed), 6)
    return {
        "grad_out": normal_values(seeds[0], (ROWS, D), 1.0, 6.0, ((0, 768),)),
        "route_weight": jnp.clip(jnp.exp(math.log(1.0) - 2.9957323 * jax.random.uniform(seeds[1], (ROWS,), jnp.float32) ** shard_levels(seeds[1], (ROWS,), ((0, 768),), -0.2, 0.2)), 0.05, 1.0),
        "counts": draw_counts(jax.random.fold_in(seeds[5], 71), 0),
        "preact": noise_with(seeds[3], (ROWS, 2 * H), 1.0, 24.0, ((0, 768),), (0, 1, 768, 6.0)),
        "down_weight": normal_values(seeds[4], (N_EXPERT, H, D), H ** -0.5, 0.21875, ((0, 8),)),
    }


def reference(grad_out, route_weight, counts, preact, down_weight):
    expert_count = N_EXPERT
    replica_count = N_EDATA
    slot_index = lax.broadcasted_iota(jnp.int32, (expert_count, replica_count, expert_count, CAP), 3)
    live_rows = (slot_index < counts.reshape(expert_count, replica_count, expert_count)[..., None]).astype(jnp.float32)
    slot_weight = route_weight.reshape(expert_count, replica_count, expert_count, CAP) * live_rows
    grad_blocks = grad_out.reshape(expert_count, replica_count, expert_count, CAP, D).transpose(2, 1, 0, 3, 4)
    weight_blocks = slot_weight.transpose(2, 1, 0, 3)
    pre_blocks = preact.reshape(expert_count, replica_count, expert_count * CAP, 2 * H)

    def per_expert(inputs):
        grad_part, weight_part, pre_part, weight_mat = inputs
        arrived_rows = (grad_part.astype(jnp.float32) * weight_part[..., None]).astype(jnp.bfloat16)
        arrived_rows = arrived_rows.reshape(replica_count * expert_count * CAP, D)
        pre_rows = pre_part.reshape(replica_count * expert_count * CAP, 2 * H)
        gate_value = pre_rows[:, :H].astype(jnp.float32)
        up_value = pre_rows[:, H:].astype(jnp.float32)
        sigmoid_gate = jax.nn.sigmoid(gate_value)
        silu_gate = gate_value * sigmoid_gate
        hidden_act = (silu_gate * up_value).astype(jnp.bfloat16)
        grad_hidden = jnp.dot(arrived_rows, weight_mat.T, preferred_element_type=jnp.float32)
        grad_gate = grad_hidden * up_value * sigmoid_gate * (1.0 + gate_value * (1.0 - sigmoid_gate))
        grad_up = grad_hidden * silu_gate
        grad_rows = jnp.concatenate([grad_gate, grad_up], axis=1).astype(jnp.bfloat16)
        row_score = jnp.sum(grad_hidden * hidden_act.astype(jnp.float32), axis=1)
        weight_sum = jnp.dot(hidden_act.T, arrived_rows, preferred_element_type=jnp.float32) / replica_count
        return grad_rows, weight_sum, row_score

    grad_rows, weight_grad, row_score = lax.map(per_expert, (grad_blocks, weight_blocks, pre_blocks, down_weight))
    grad_preact = grad_rows.reshape(ROWS, 2 * H)
    score_blocks = row_score.reshape(expert_count, replica_count, expert_count, CAP).transpose(2, 1, 0, 3)
    route_grad = live_rows * score_blocks / route_weight.reshape(expert_count, replica_count, expert_count, CAP)
    return grad_preact, weight_grad, route_grad.reshape(ROWS)
```

```python
import jax
import jax.numpy as jnp
from jax import lax
from jax.sharding import Mesh, PartitionSpec as P

EXPERT = ("yh", "x")
EDATA = ("y1", "y0", "zz", "z0", "core")
DEVICE = EXPERT + EDATA


def swap(value, axis):
    return lax.ppermute(value, axis, [(0, 1), (1, 0)])


def pick(value, index, axis):
    return lax.dynamic_index_in_dim(value, index, axis, keepdims=False)


def body(grad_out, route_weight, counts, preact, down_weight):
    row_total, feature_count = grad_out.shape
    expert_count = lax.axis_size(EXPERT)
    capacity = row_total // expert_count
    hidden_count = down_weight.shape[1]
    half = feature_count // 2
    quarter = half // 2
    replica_count = lax.axis_size(EDATA)
    core = lax.axis_index("core")
    z0 = lax.axis_index("z0")
    y0 = lax.axis_index("y0")
    size_y1, size_zz = lax.axis_size("y1"), lax.axis_size("zz")
    unit = hidden_count // (replica_count // 2)

    slot_index = lax.broadcasted_iota(jnp.int32, (expert_count, capacity), 1)
    live_rows = (slot_index < counts[:, None]).astype(jnp.float32)
    route_matrix = route_weight.reshape(expert_count, capacity)
    slot_weight = route_matrix * live_rows

    gate_value = preact[:, :hidden_count].astype(jnp.float32)
    up_value = preact[:, hidden_count:].astype(jnp.float32)
    sigmoid_gate = jax.nn.sigmoid(gate_value)
    silu_gate = gate_value * sigmoid_gate
    hidden_act = (silu_gate * up_value).astype(jnp.bfloat16)
    hidden_blocks = hidden_act.reshape(expert_count, capacity, hidden_count)
    other_blocks = swap(hidden_blocks, "core")

    scaled_rows = (
        grad_out.reshape(expert_count, capacity, feature_count) * slot_weight[:, :, None]
    ).astype(jnp.bfloat16)
    outgoing = jnp.stack([scaled_rows[:, :, :half], scaled_rows[:, :, half:]], axis=1)
    arrived = lax.all_to_all(
        outgoing.reshape(expert_count * 2, capacity, half),
        EXPERT + ("core",), split_axis=0, concat_axis=0, tiled=True,
    ).reshape(expert_count, 2, capacity, half)

    first_core = core == 0
    hidden_all = jnp.stack(
        [
            jnp.where(first_core, hidden_blocks, other_blocks),
            jnp.where(first_core, other_blocks, hidden_blocks),
        ],
        axis=1,
    ).reshape(2 * row_total, hidden_count)
    partial_sum = lax.dot_general(
        hidden_all, arrived.reshape(2 * row_total, half), (((0,), (0,)), ((), ())),
        preferred_element_type=jnp.float32,
    )
    parts = partial_sum.reshape(size_y1, 2, size_zz, 2, unit, half)
    part_a, part_b = parts[..., :quarter], parts[..., quarter:]
    sent_a = pick(part_a, 1 - z0, 3).astype(jnp.bfloat16)
    sent_b = pick(part_b, 1 - y0, 1).astype(jnp.bfloat16)
    came_a = swap(sent_a, "z0")
    came_b = swap(sent_b, "y0")

    arrived, sent_a, sent_b = lax.optimization_barrier((arrived, sent_a, sent_b))
    weight_half = lax.dynamic_slice(
        down_weight[0], (0, core * half), (hidden_count, half)
    )
    grad_partial = lax.dot_general(
        arrived.reshape(2 * row_total, half), weight_half, (((1,), (1,)), ((), ())),
        preferred_element_type=jnp.float32,
    ).reshape(expert_count, 2, capacity, hidden_count)
    grad_other = swap(pick(grad_partial, 1 - core, 1), "core")
    grad_hidden = (pick(grad_partial, core, 1) + grad_other).reshape(row_total, hidden_count)
    grad_gate = grad_hidden * up_value * sigmoid_gate * (1.0 + gate_value * (1.0 - sigmoid_gate))
    grad_up = grad_hidden * silu_gate
    grad_rows = jnp.concatenate([grad_gate, grad_up], axis=1).astype(jnp.bfloat16)
    row_score = jnp.sum(grad_hidden * hidden_act.astype(jnp.float32), axis=1)
    returned_score = lax.all_to_all(
        row_score.reshape(expert_count, capacity), EXPERT, split_axis=0, concat_axis=0, tiled=True
    )
    route_grad = live_rows * returned_score / route_matrix

    sum_a = pick(part_a, z0, 3) + came_a.astype(jnp.float32)
    sum_b = pick(part_b, y0, 1) + came_b.astype(jnp.float32)
    sent_a = pick(sum_a, 1 - y0, 1).astype(jnp.bfloat16)
    sent_b = pick(sum_b, 1 - z0, 2).astype(jnp.bfloat16)
    came_a = swap(sent_a, "y0")
    came_b = swap(sent_b, "z0")
    sum_a = pick(sum_a, y0, 1) + came_a.astype(jnp.float32)
    sum_b = pick(sum_b, z0, 2) + came_b.astype(jnp.float32)
    spread = jnp.concatenate([sum_a, sum_b], axis=-1).astype(jnp.bfloat16)
    gathered = lax.all_to_all(
        spread.reshape(size_y1 * size_zz * 2, unit // 2, half),
        ("y1", "zz", "core"), split_axis=0, concat_axis=0, tiled=True,
    ).reshape(size_y1 * size_zz, 2, unit // 2, half)
    total = jnp.sum(gathered.astype(jnp.float32), axis=0) / replica_count
    weight_grad = jnp.concatenate([total[0], total[1]], axis=1)[None]
    return (grad_rows, weight_grad, route_grad.reshape(row_total))


def solution(mesh):
    fine = Mesh(mesh.devices.reshape(2, 4, 2, 2, 6, 2, 2), DEVICE)
    in_specs = (P(DEVICE, None), P(DEVICE), P(DEVICE), P(DEVICE, None), P(EXPERT, None, None))
    out_specs = (P(DEVICE, None), P(EXPERT, EDATA, None), P(DEVICE))
    return jax.shard_map(body, mesh=fine, in_specs=in_specs, out_specs=out_specs, check_vma=False)
```

```python
import jax
import jax.numpy as jnp
from jax import lax
from jax.sharding import Mesh, PartitionSpec as P

EXPERT = ("yh", "x")
EDATA = ("y1", "y0", "zc", "z1", "z0", "core")
ROWS = ("y1", "y0", "zc", "z1", "z0")
DEVICE = EXPERT + EDATA


def swap(value, axis):
    return lax.ppermute(value, axis, [(0, 1), (1, 0)])


def pick(value, index, axis):
    return lax.dynamic_index_in_dim(value, index, axis, keepdims=False)


class Piece:
    def __init__(self, value, dims):
        self.value, self.dims = value, dims

    def send(self, axis):
        self.axis, self.at = axis, self.dims.index(axis)
        self.sent = pick(self.value, 1 - lax.axis_index(axis), self.at).astype(jnp.bfloat16)
        self.came = swap(self.sent, axis)

    def receive(self):
        self.value = pick(self.value, lax.axis_index(self.axis), self.at) + self.came.astype(jnp.float32)
        self.dims = self.dims[: self.at] + self.dims[self.at + 1 :]


def body(grad_out, route_weight, counts, preact, down_weight):
    row_total, feature_count = grad_out.shape
    expert_count = lax.axis_size(EXPERT)
    capacity = row_total // expert_count
    hidden_count = down_weight.shape[1]
    half = feature_count // 2
    quarter = half // 2
    replica_count = lax.axis_size(EDATA)
    core = lax.axis_index("core")
    cube_count = lax.axis_size("zc")
    unit = hidden_count // (replica_count // 2)

    slot_index = lax.broadcasted_iota(jnp.int32, (expert_count, capacity), 1)
    live_rows = (slot_index < counts[:, None]).astype(jnp.float32)
    route_matrix = route_weight.reshape(expert_count, capacity)
    slot_weight = route_matrix * live_rows

    gate_value = preact[:, :hidden_count].astype(jnp.float32)
    up_value = preact[:, hidden_count:].astype(jnp.float32)
    sigmoid_gate = jax.nn.sigmoid(gate_value)
    silu_gate = gate_value * sigmoid_gate
    hidden_act = (silu_gate * up_value).astype(jnp.bfloat16)
    hidden_blocks = hidden_act.reshape(expert_count, capacity, hidden_count)
    other_blocks = swap(hidden_blocks, "core")

    scaled_rows = (
        grad_out.reshape(expert_count, capacity, feature_count) * slot_weight[:, :, None]
    ).astype(jnp.bfloat16)
    outgoing = jnp.stack([scaled_rows[:, :, :half], scaled_rows[:, :, half:]], axis=1)
    arrived = lax.all_to_all(
        outgoing.reshape(expert_count * 2, capacity, half),
        EXPERT + ("core",), split_axis=0, concat_axis=0, tiled=True,
    ).reshape(expert_count, 2, capacity, half)

    first_core = core == 0
    hidden_all = jnp.stack(
        [
            jnp.where(first_core, hidden_blocks, other_blocks),
            jnp.where(first_core, other_blocks, hidden_blocks),
        ],
        axis=1,
    ).reshape(2 * row_total, hidden_count)
    partial_sum = lax.dot_general(
        hidden_all, arrived.reshape(2 * row_total, half), (((0,), (0,)), ((), ())),
        preferred_element_type=jnp.float32,
    )
    parts = partial_sum.reshape([lax.axis_size(axis) for axis in ROWS] + [unit, half])
    piece_a, piece_b = Piece(parts[..., :quarter], ROWS), Piece(parts[..., quarter:], ROWS)
    piece_a.send("z0")
    piece_b.send("y0")

    arrived, _, _ = lax.optimization_barrier((arrived, piece_a.sent, piece_b.sent))
    weight_half = lax.dynamic_slice(
        down_weight[0], (0, core * half), (hidden_count, half)
    )
    grad_partial = lax.dot_general(
        arrived.reshape(2 * row_total, half), weight_half, (((1,), (1,)), ((), ())),
        preferred_element_type=jnp.float32,
    ).reshape(expert_count, 2, capacity, hidden_count)
    grad_other = swap(pick(grad_partial, 1 - core, 1), "core")
    grad_hidden = (pick(grad_partial, core, 1) + grad_other).reshape(row_total, hidden_count)
    grad_gate = grad_hidden * up_value * sigmoid_gate * (1.0 + gate_value * (1.0 - sigmoid_gate))
    grad_up = grad_hidden * silu_gate
    grad_rows = jnp.concatenate([grad_gate, grad_up], axis=1).astype(jnp.bfloat16)
    row_score = jnp.sum(grad_hidden * hidden_act.astype(jnp.float32), axis=1)
    for next_a, next_b in (("y0", "z0"), ("z1", "y1"), ("y1", "z1"), (None, None)):
        if next_a == "z1":
            piece_a.came, row_score = lax.optimization_barrier((piece_a.came, row_score))
        piece_a.receive()
        piece_b.receive()
        if next_a is not None:
            piece_a.send(next_a)
            piece_b.send(next_b)
    returned_score = lax.all_to_all(
        row_score.reshape(expert_count, capacity), EXPERT, split_axis=0, concat_axis=0, tiled=True
    )
    route_grad = live_rows * returned_score / route_matrix

    spread = jnp.concatenate([piece_a.value, piece_b.value], axis=-1).astype(jnp.bfloat16)
    gathered = lax.all_to_all(
        spread.reshape(cube_count * 2, unit // 2, half),
        ("zc", "core"), split_axis=0, concat_axis=0, tiled=True,
    ).reshape(cube_count, 2, unit // 2, half)
    total = jnp.sum(gathered.astype(jnp.float32), axis=0) / replica_count
    weight_grad = jnp.concatenate([total[0], total[1]], axis=1)[None]
    return (grad_rows, weight_grad, route_grad.reshape(row_total))


def solution(mesh):
    fine = Mesh(mesh.devices.reshape(2, 4, 2, 2, 3, 2, 2, 2), DEVICE)
    in_specs = (P(DEVICE, None), P(DEVICE), P(DEVICE), P(DEVICE, None), P(EXPERT, None, None))
    out_specs = (P(DEVICE, None), P(EXPERT, EDATA, None), P(DEVICE))
    return jax.shard_map(body, mesh=fine, in_specs=in_specs, out_specs=out_specs, check_vma=False)
```

```python
import jax
import jax.numpy as jnp
from jax import lax
from jax.experimental import pallas as pl
from jax.experimental.pallas import tpu as pltpu
from jax.sharding import Mesh, PartitionSpec as P

EXPERT = ("yh", "x")
EDATA = ("y1", "y0", "zc", "z1", "z0", "core")
DEVICE = EXPERT + EDATA
CUBE = ("y1", "y0", "z1", "z0", "core")
STAGES = (("z0", "y0"), ("y0", "z0"), ("z1", "y1"), ("y1", "z1"))


def swap(value, axis):
    return lax.ppermute(value, axis, [(0, 1), (1, 0)])


def pick(value, index, axis):
    return lax.dynamic_index_in_dim(value, index, axis, keepdims=False)


def stage_pairs(stage):
    pairs = []
    for source in range(32):
        axis = STAGES[stage][source % 2]
        pairs.append((source, source ^ (16 >> CUBE.index(axis))))
    return pairs


def block_order(cube_count):
    block = jnp.arange(16 * cube_count, dtype=jnp.int32)
    cube = block % cube_count
    orders = []
    for core in range(2):
        place = {}
        for stage in range(4):
            axis = STAGES[stage][core]
            place[axis] = lax.axis_index(axis) ^ (block // cube_count // (8 >> stage) % 2)
        orders.append(
            (((place["y1"] * 2 + place["y0"]) * cube_count + cube) * 2 + place["z1"]) * 2 + place["z0"]
        )
    return jnp.where(lax.axis_index("core") == 0, orders[0], orders[1]).astype(jnp.int32)


def reorder_kernel(order_ref, source_ref, out_ref):
    count = order_ref.shape[0]
    unit = source_ref.shape[0] // count
    for block in range(count):
        start = pl.multiple_of(order_ref[block] * unit, unit)
        out_ref[block * unit : (block + 1) * unit, :] = source_ref[pl.ds(start, unit), :]


def reorder(source, order):
    return pl.pallas_call(
        reorder_kernel,
        out_shape=jax.ShapeDtypeStruct(source.shape, source.dtype),
        in_specs=[pl.BlockSpec(memory_space=pltpu.SMEM), pl.BlockSpec(memory_space=pltpu.VMEM)],
        out_specs=pl.BlockSpec(memory_space=pltpu.VMEM),
        compiler_params=pltpu.CompilerParams(vmem_limit_bytes=16 * 2**20),
        cost_estimate=pl.CostEstimate(flops=0, bytes_accessed=2 * 2 * source.size, transcendentals=0),
    )(order, source)


def scale_kernel(counts_ref, route_ref, grad_ref, out_ref):
    step = pl.program_id(0)
    blocks, _, capacity, half = out_ref.shape
    slots = route_ref.shape[1]
    slot = lax.broadcasted_iota(jnp.int32, (capacity, slots), 1)
    row = lax.broadcasted_iota(jnp.int32, (capacity, slots), 0)
    for block in range(blocks):
        expert = step * blocks + block
        own = (slot == row + expert * capacity) & (row < counts_ref[expert])
        slot_weight = jnp.sum(jnp.where(own, route_ref[...], 0.0), axis=1, keepdims=True)
        rows = grad_ref[block * capacity : (block + 1) * capacity, :].astype(jnp.float32) * slot_weight
        rows = rows.astype(jnp.bfloat16)
        out_ref[block, 0] = rows[:, :half]
        out_ref[block, 1] = rows[:, half:]


def scale(counts, route_weight, grad_out):
    row_total, feature_count = grad_out.shape
    expert_count = counts.shape[0]
    capacity = row_total // expert_count
    half = feature_count // 2
    blocks = 2
    return pl.pallas_call(
        scale_kernel,
        grid=(expert_count // blocks,),
        out_shape=jax.ShapeDtypeStruct((expert_count, 2, capacity, half), jnp.bfloat16),
        in_specs=[
            pl.BlockSpec(memory_space=pltpu.SMEM),
            pl.BlockSpec((1, row_total), lambda step: (0, 0)),
            pl.BlockSpec((blocks * capacity, feature_count), lambda step: (step, 0)),
        ],
        out_specs=pl.BlockSpec((blocks, 2, capacity, half), lambda step: (step, 0, 0, 0)),
        compiler_params=pltpu.CompilerParams(vmem_limit_bytes=16 * 2**20),
        cost_estimate=pl.CostEstimate(
            flops=grad_out.size, bytes_accessed=4 * grad_out.size, transcendentals=0
        ),
    )(counts, route_weight.reshape(1, row_total), grad_out)


def body(grad_out, route_weight, counts, preact, down_weight):
    row_total, feature_count = grad_out.shape
    expert_count = lax.axis_size(EXPERT)
    capacity = row_total // expert_count
    hidden_count = down_weight.shape[1]
    half = feature_count // 2
    replica_count = lax.axis_size(EDATA)
    core = lax.axis_index("core")
    cube_count = lax.axis_size("zc")

    outgoing = scale(counts, route_weight, grad_out)
    arrived = lax.all_to_all(
        outgoing.reshape(expert_count * 2, capacity, half),
        EXPERT + ("core",), split_axis=0, concat_axis=0, tiled=True,
    ).reshape(expert_count, 2, capacity, half)

    gate_value = preact[:, :hidden_count].astype(jnp.float32)
    up_value = preact[:, hidden_count:].astype(jnp.float32)
    sigmoid_gate = jax.nn.sigmoid(gate_value)
    silu_gate = gate_value * sigmoid_gate
    hidden_act = (silu_gate * up_value).astype(jnp.bfloat16)
    hidden_blocks = hidden_act.reshape(expert_count, capacity, hidden_count)
    other_blocks = swap(hidden_blocks, "core")
    first_core = core == 0
    hidden_all = jnp.stack(
        [
            jnp.where(first_core, hidden_blocks, other_blocks),
            jnp.where(first_core, other_blocks, hidden_blocks),
        ],
        axis=1,
    ).reshape(2 * row_total, hidden_count)
    hidden_units = reorder(hidden_all.T, block_order(cube_count))

    def product(units, rows):
        return lax.dot_general(
            units, rows.reshape(2 * row_total, half), (((1,), (0,)), ((), ())),
            preferred_element_type=jnp.float32,
        )

    rows_left = hidden_count // 2
    sent = product(hidden_units[rows_left:], arrived).astype(jnp.bfloat16)
    came = lax.ppermute(sent, CUBE, stage_pairs(0))
    arrived, _ = lax.optimization_barrier((arrived, sent))
    kept = product(hidden_units[:rows_left], arrived)
    came, kept = lax.optimization_barrier((came, kept))

    weight_half = lax.dynamic_slice(
        down_weight[0], (0, core * half), (hidden_count, half)
    )
    grad_partial = lax.dot_general(
        arrived.reshape(2 * row_total, half), weight_half, (((1,), (1,)), ((), ())),
        preferred_element_type=jnp.float32,
    ).reshape(expert_count, 2, capacity, hidden_count)
    grad_other = swap(pick(grad_partial, 1 - core, 1), "core")
    grad_hidden = (pick(grad_partial, core, 1) + grad_other).reshape(row_total, hidden_count)
    grad_gate = grad_hidden * up_value * sigmoid_gate * (1.0 + gate_value * (1.0 - sigmoid_gate))
    grad_up = grad_hidden * silu_gate
    grad_rows = jnp.concatenate([grad_gate, grad_up], axis=1).astype(jnp.bfloat16)
    row_score = jnp.sum(grad_hidden * hidden_act.astype(jnp.float32), axis=1)

    for stage in range(1, 4):
        total = kept + came.astype(jnp.float32)
        rows_left //= 2
        sent = total[rows_left:].astype(jnp.bfloat16)
        kept = total[:rows_left]
        came = lax.ppermute(sent, CUBE, stage_pairs(stage))
        if stage == 1:
            came, row_score = lax.optimization_barrier((came, row_score))
            returned_score = lax.all_to_all(
                row_score.reshape(expert_count, capacity), EXPERT, split_axis=0, concat_axis=0, tiled=True
            )
    slot_index = lax.broadcasted_iota(jnp.int32, (expert_count, capacity), 1)
    live_rows = (slot_index < counts[:, None]).astype(jnp.float32)
    route_grad = live_rows * returned_score / route_weight.reshape(expert_count, capacity)

    spread = (kept + came.astype(jnp.float32)).astype(jnp.bfloat16)
    gathered = lax.all_to_all(
        spread.reshape(cube_count * 2, rows_left // (2 * cube_count), half),
        ("zc", "core"), split_axis=0, concat_axis=0, tiled=True,
    ).reshape(cube_count, 2, rows_left // (2 * cube_count), half)
    total = jnp.sum(gathered.astype(jnp.float32), axis=0) / replica_count
    weight_grad = jnp.concatenate([total[0], total[1]], axis=1)[None]
    return (grad_rows, weight_grad, route_grad.reshape(row_total))


def solution(mesh):
    fine = Mesh(mesh.devices.reshape(2, 4, 2, 2, 3, 2, 2, 2), DEVICE)
    in_specs = (P(DEVICE, None), P(DEVICE), P(DEVICE), P(DEVICE, None), P(EXPERT, None, None))
    out_specs = (P(DEVICE, None), P(EXPERT, EDATA, None), P(DEVICE))
    return jax.shard_map(body, mesh=fine, in_specs=in_specs, out_specs=out_specs, check_vma=False)
```

```python
import jax
import jax.numpy as jnp
from jax import lax
from jax.experimental import pallas as pl
from jax.experimental.pallas import tpu as pltpu
from jax.sharding import Mesh, PartitionSpec as P

EXPERT = ("yh", "x")
EDATA = ("y1", "y0", "zc", "z1", "z0", "core")
DEVICE = EXPERT + EDATA
CUBE = ("y1", "y0", "z1", "z0", "core")
STAGES = (("z0", "y0"), ("y0", "z0"))
REST = ("y1", "zc", "z1", "core")


def swap(value, axis):
    return lax.ppermute(value, axis, [(0, 1), (1, 0)])


def pick(value, index, axis):
    return lax.dynamic_index_in_dim(value, index, axis, keepdims=False)


def stage_pairs(stage):
    pairs = []
    for source in range(32):
        axis = STAGES[stage][source % 2]
        pairs.append((source, source ^ (16 >> CUBE.index(axis))))
    return pairs


def block_order(cube_count):
    rest = 4 * cube_count
    block = jnp.arange(4 * rest, dtype=jnp.int32)
    place_y1, place_cube, place_z1 = block % rest // (rest // 2), block % (rest // 2) // 2, block % 2
    orders = []
    for core in range(2):
        place = {}
        for stage in range(2):
            axis = STAGES[stage][core]
            place[axis] = lax.axis_index(axis) ^ (block // rest // (2 >> stage) % 2)
        orders.append(
            (((place_y1 * 2 + place["y0"]) * cube_count + place_cube) * 2 + place_z1) * 2 + place["z0"]
        )
    return jnp.where(lax.axis_index("core") == 0, orders[0], orders[1]).astype(jnp.int32)


def reorder_kernel(order_ref, source_ref, out_ref):
    count = order_ref.shape[0]
    unit = source_ref.shape[0] // count
    for block in range(count):
        start = pl.multiple_of(order_ref[block] * unit, unit)
        out_ref[block * unit : (block + 1) * unit, :] = source_ref[pl.ds(start, unit), :]


def reorder(source, order):
    return pl.pallas_call(
        reorder_kernel,
        out_shape=jax.ShapeDtypeStruct(source.shape, source.dtype),
        in_specs=[pl.BlockSpec(memory_space=pltpu.SMEM), pl.BlockSpec(memory_space=pltpu.VMEM)],
        out_specs=pl.BlockSpec(memory_space=pltpu.VMEM),
        compiler_params=pltpu.CompilerParams(vmem_limit_bytes=16 * 2**20),
        cost_estimate=pl.CostEstimate(flops=0, bytes_accessed=2 * 2 * source.size, transcendentals=0),
    )(order, source)


def scale_kernel(counts_ref, route_ref, grad_ref, out_ref):
    step = pl.program_id(0)
    blocks, _, capacity, half = out_ref.shape
    slots = route_ref.shape[1]
    slot = lax.broadcasted_iota(jnp.int32, (capacity, slots), 1)
    row = lax.broadcasted_iota(jnp.int32, (capacity, slots), 0)
    for block in range(blocks):
        expert = step * blocks + block
        own = (slot == row + expert * capacity) & (row < counts_ref[expert])
        slot_weight = jnp.sum(jnp.where(own, route_ref[...], 0.0), axis=1, keepdims=True)
        rows = grad_ref[block * capacity : (block + 1) * capacity, :].astype(jnp.float32) * slot_weight
        rows = rows.astype(jnp.bfloat16)
        out_ref[block, 0] = rows[:, :half]
        out_ref[block, 1] = rows[:, half:]


def scale(counts, route_weight, grad_out):
    row_total, feature_count = grad_out.shape
    expert_count = counts.shape[0]
    capacity = row_total // expert_count
    half = feature_count // 2
    blocks = 2
    return pl.pallas_call(
        scale_kernel,
        grid=(expert_count // blocks,),
        out_shape=jax.ShapeDtypeStruct((expert_count, 2, capacity, half), jnp.bfloat16),
        in_specs=[
            pl.BlockSpec(memory_space=pltpu.SMEM),
            pl.BlockSpec((1, row_total), lambda step: (0, 0)),
            pl.BlockSpec((blocks * capacity, feature_count), lambda step: (step, 0)),
        ],
        out_specs=pl.BlockSpec((blocks, 2, capacity, half), lambda step: (step, 0, 0, 0)),
        compiler_params=pltpu.CompilerParams(vmem_limit_bytes=60 * 2**20),
        cost_estimate=pl.CostEstimate(
            flops=grad_out.size, bytes_accessed=4 * grad_out.size, transcendentals=0
        ),
    )(counts, route_weight.reshape(1, row_total), grad_out)


def body(grad_out, route_weight, counts, preact, down_weight):
    row_total, feature_count = grad_out.shape
    expert_count = lax.axis_size(EXPERT)
    capacity = row_total // expert_count
    hidden_count = down_weight.shape[1]
    half = feature_count // 2
    replica_count = lax.axis_size(EDATA)
    core = lax.axis_index("core")
    cube_count = lax.axis_size("zc")

    outgoing = scale(counts, route_weight, grad_out)
    arrived = lax.all_to_all(
        outgoing.reshape(expert_count * 2, capacity, half),
        EXPERT + ("core",), split_axis=0, concat_axis=0, tiled=True,
    ).reshape(expert_count, 2, capacity, half)

    gate_value = preact[:, :hidden_count].astype(jnp.float32)
    up_value = preact[:, hidden_count:].astype(jnp.float32)
    sigmoid_gate = jax.nn.sigmoid(gate_value)
    silu_gate = gate_value * sigmoid_gate
    hidden_act = (silu_gate * up_value).astype(jnp.bfloat16)
    hidden_blocks = hidden_act.reshape(expert_count, capacity, hidden_count)
    other_blocks = swap(hidden_blocks, "core")
    first_core = core == 0
    hidden_all = jnp.stack(
        [
            jnp.where(first_core, hidden_blocks, other_blocks),
            jnp.where(first_core, other_blocks, hidden_blocks),
        ],
        axis=1,
    ).reshape(2 * row_total, hidden_count)
    hidden_units = reorder(hidden_all.T, block_order(cube_count))

    def product(units, rows):
        return lax.dot_general(
            units, rows.reshape(2 * row_total, half), (((1,), (0,)), ((), ())),
            preferred_element_type=jnp.float32,
        )

    rows_left = hidden_count // 2
    sent = product(hidden_units[rows_left:], arrived).astype(jnp.bfloat16)
    came = lax.ppermute(sent, CUBE, stage_pairs(0))
    arrived, _ = lax.optimization_barrier((arrived, sent))
    kept = product(hidden_units[:rows_left], arrived)

    weight_half = lax.dynamic_slice(
        down_weight[0], (0, core * half), (hidden_count, half)
    )
    grad_partial = lax.dot_general(
        arrived.reshape(2 * row_total, half), weight_half, (((1,), (1,)), ((), ())),
        preferred_element_type=jnp.float32,
    ).reshape(expert_count, 2, capacity, hidden_count)
    grad_other = swap(pick(grad_partial, 1 - core, 1), "core")
    grad_hidden = (pick(grad_partial, core, 1) + grad_other).reshape(row_total, hidden_count)
    grad_gate = grad_hidden * up_value * sigmoid_gate * (1.0 + gate_value * (1.0 - sigmoid_gate))
    grad_up = grad_hidden * silu_gate
    grad_rows = jnp.concatenate([grad_gate, grad_up], axis=1).astype(jnp.bfloat16)
    row_score = jnp.sum(grad_hidden * hidden_act.astype(jnp.float32), axis=1)

    came, kept = lax.optimization_barrier((came, kept))
    total = kept + came.astype(jnp.float32)
    rows_left //= 2
    sent = total[rows_left:].astype(jnp.bfloat16)
    kept = total[:rows_left]
    came = lax.ppermute(sent, CUBE, stage_pairs(1))
    came, row_score = lax.optimization_barrier((came, row_score))
    spread = (kept + came.astype(jnp.float32)).astype(jnp.bfloat16)
    unit = rows_left // lax.axis_size(REST)
    spread, row_score = lax.optimization_barrier((spread, row_score))
    gathered = lax.all_to_all(
        spread.reshape(-1, unit, half), REST, split_axis=0, concat_axis=0, tiled=True
    ).reshape(-1, 2, unit, half)
    all_scores = lax.all_gather(row_score.reshape(expert_count, capacity), EXPERT)
    returned_score = pick(all_scores, lax.axis_index(EXPERT), 1)
    slot_index = lax.broadcasted_iota(jnp.int32, (expert_count, capacity), 1)
    live_rows = (slot_index < counts[:, None]).astype(jnp.float32)
    route_grad = live_rows * returned_score / route_weight.reshape(expert_count, capacity)

    total = jnp.sum(gathered.astype(jnp.float32), axis=0) / replica_count
    weight_grad = jnp.concatenate([total[0], total[1]], axis=1)[None]
    return (grad_rows, weight_grad, route_grad.reshape(row_total))


def solution(mesh):
    fine = Mesh(mesh.devices.reshape(2, 4, 2, 2, 3, 2, 2, 2), DEVICE)
    in_specs = (P(DEVICE, None), P(DEVICE), P(DEVICE), P(DEVICE, None), P(EXPERT, None, None))
    out_specs = (P(DEVICE, None), P(EXPERT, EDATA, None), P(DEVICE))
    return jax.shard_map(body, mesh=fine, in_specs=in_specs, out_specs=out_specs, check_vma=False)
```

```python
import jax
import jax.numpy as jnp
from jax import lax
from jax.experimental import pallas as pl
from jax.experimental.pallas import tpu as pltpu
from jax.sharding import Mesh, PartitionSpec as P

EXPERT = ("yh", "x")
EDATA = ("y1", "y0", "zc", "z1", "z0", "core")
DEVICE = EXPERT + EDATA
CUBE = ("y1", "y0", "z1", "z0", "core")
STAGES = (("z0", "y0"), ("y0", "z0"))
REST = ("y1", "zc", "z1", "core")


def swap(value, axis):
    return lax.ppermute(value, axis, [(0, 1), (1, 0)])


def pick(value, index, axis):
    return lax.dynamic_index_in_dim(value, index, axis, keepdims=False)


def send_back(score):
    capacity = score.shape[1]
    score = score.reshape(2, 2, 2, 1, capacity)
    for axis, bit in (("yh", 1), ("x", 2), ("x", 1)):
        mine = lax.axis_index(axis) // bit % 2
        size = lax.axis_size(axis)
        kept = pick(score, mine, 0)
        came = lax.ppermute(pick(score, 1 - mine, 0), axis, [(i, i ^ bit) for i in range(size)])
        both = jnp.where(mine == 0, jnp.stack([kept, came], -2), jnp.stack([came, kept], -2))
        score = both.reshape(kept.shape[:-2] + (-1, capacity))
    return score


def stage_pairs(stage):
    pairs = []
    for source in range(32):
        axis = STAGES[stage][source % 2]
        pairs.append((source, source ^ (16 >> CUBE.index(axis))))
    return pairs


def block_order(cube_count):
    rest = 4 * cube_count
    block = jnp.arange(4 * rest, dtype=jnp.int32)
    place_y1, place_cube, place_z1 = block % rest // (rest // 2), block % (rest // 2) // 2, block % 2
    orders = []
    for core in range(2):
        place = {}
        for stage in range(2):
            axis = STAGES[stage][core]
            place[axis] = lax.axis_index(axis) ^ (block // rest // (2 >> stage) % 2)
        orders.append(
            (((place_y1 * 2 + place["y0"]) * cube_count + place_cube) * 2 + place_z1) * 2 + place["z0"]
        )
    return jnp.where(lax.axis_index("core") == 0, orders[0], orders[1]).astype(jnp.int32)


def reorder_kernel(order_ref, source_ref, out_ref):
    count = order_ref.shape[0]
    unit = source_ref.shape[0] // count
    for block in range(count):
        start = pl.multiple_of(order_ref[block] * unit, unit)
        out_ref[block * unit : (block + 1) * unit, :] = source_ref[pl.ds(start, unit), :]


def reorder(source, order):
    return pl.pallas_call(
        reorder_kernel,
        out_shape=jax.ShapeDtypeStruct(source.shape, source.dtype),
        in_specs=[pl.BlockSpec(memory_space=pltpu.SMEM), pl.BlockSpec(memory_space=pltpu.VMEM)],
        out_specs=pl.BlockSpec(memory_space=pltpu.VMEM),
        compiler_params=pltpu.CompilerParams(vmem_limit_bytes=16 * 2**20),
        cost_estimate=pl.CostEstimate(flops=0, bytes_accessed=2 * 2 * source.size, transcendentals=0),
    )(order, source)


def scale_kernel(counts_ref, route_ref, grad_ref, out_ref):
    step = pl.program_id(0)
    blocks, _, capacity, half = out_ref.shape
    slots = route_ref.shape[1]
    slot = lax.broadcasted_iota(jnp.int32, (capacity, slots), 1)
    row = lax.broadcasted_iota(jnp.int32, (capacity, slots), 0)
    for block in range(blocks):
        expert = step * blocks + block
        own = (slot == row + expert * capacity) & (row < counts_ref[expert])
        slot_weight = jnp.sum(jnp.where(own, route_ref[...], 0.0), axis=1, keepdims=True)
        rows = grad_ref[block * capacity : (block + 1) * capacity, :].astype(jnp.float32) * slot_weight
        rows = rows.astype(jnp.bfloat16)
        out_ref[block, 0] = rows[:, :half]
        out_ref[block, 1] = rows[:, half:]


def scale(counts, route_weight, grad_out):
    row_total, feature_count = grad_out.shape
    expert_count = counts.shape[0]
    capacity = row_total // expert_count
    half = feature_count // 2
    blocks = 2
    return pl.pallas_call(
        scale_kernel,
        grid=(expert_count // blocks,),
        out_shape=jax.ShapeDtypeStruct((expert_count, 2, capacity, half), jnp.bfloat16),
        in_specs=[
            pl.BlockSpec(memory_space=pltpu.SMEM),
            pl.BlockSpec((1, row_total), lambda step: (0, 0)),
            pl.BlockSpec((blocks * capacity, feature_count), lambda step: (step, 0)),
        ],
        out_specs=pl.BlockSpec((blocks, 2, capacity, half), lambda step: (step, 0, 0, 0)),
        compiler_params=pltpu.CompilerParams(vmem_limit_bytes=60 * 2**20),
        cost_estimate=pl.CostEstimate(
            flops=grad_out.size, bytes_accessed=4 * grad_out.size, transcendentals=0
        ),
    )(counts, route_weight.reshape(1, row_total), grad_out)


def body(grad_out, route_weight, counts, preact, down_weight):
    row_total, feature_count = grad_out.shape
    expert_count = lax.axis_size(EXPERT)
    capacity = row_total // expert_count
    hidden_count = down_weight.shape[1]
    half = feature_count // 2
    replica_count = lax.axis_size(EDATA)
    core = lax.axis_index("core")
    cube_count = lax.axis_size("zc")

    outgoing = scale(counts, route_weight, grad_out)
    arrived = lax.all_to_all(
        outgoing.reshape(expert_count * 2, capacity, half),
        EXPERT + ("core",), split_axis=0, concat_axis=0, tiled=True,
    ).reshape(expert_count, 2, capacity, half)

    gate_value = preact[:, :hidden_count].astype(jnp.float32)
    up_value = preact[:, hidden_count:].astype(jnp.float32)
    sigmoid_gate = jax.nn.sigmoid(gate_value)
    silu_gate = gate_value * sigmoid_gate
    hidden_act = (silu_gate * up_value).astype(jnp.bfloat16)
    hidden_blocks = hidden_act.reshape(expert_count, capacity, hidden_count)
    other_blocks = swap(hidden_blocks, "core")
    first_core = core == 0
    hidden_all = jnp.stack(
        [
            jnp.where(first_core, hidden_blocks, other_blocks),
            jnp.where(first_core, other_blocks, hidden_blocks),
        ],
        axis=1,
    ).reshape(2 * row_total, hidden_count)
    hidden_units = reorder(hidden_all.T, block_order(cube_count))

    def product(units, rows):
        return lax.dot_general(
            units, rows.reshape(2 * row_total, half), (((1,), (0,)), ((), ())),
            preferred_element_type=jnp.float32,
        )

    rows_left = hidden_count // 2
    sent = product(hidden_units[rows_left:], arrived).astype(jnp.bfloat16)
    came = lax.ppermute(sent, CUBE, stage_pairs(0))
    arrived, _ = lax.optimization_barrier((arrived, sent))
    kept = product(hidden_units[:rows_left], arrived)

    weight_half = lax.dynamic_slice(
        down_weight[0], (0, core * half), (hidden_count, half)
    )
    grad_partial = lax.dot_general(
        arrived.reshape(2 * row_total, half), weight_half, (((1,), (1,)), ((), ())),
        preferred_element_type=jnp.float32,
    ).reshape(expert_count, 2, capacity, hidden_count)
    grad_other = swap(pick(grad_partial, 1 - core, 1), "core")
    grad_hidden = (pick(grad_partial, core, 1) + grad_other).reshape(row_total, hidden_count)
    grad_gate = grad_hidden * up_value * sigmoid_gate * (1.0 + gate_value * (1.0 - sigmoid_gate))
    grad_up = grad_hidden * silu_gate
    grad_rows = jnp.concatenate([grad_gate, grad_up], axis=1).astype(jnp.bfloat16)
    row_score = jnp.sum(grad_hidden * hidden_act.astype(jnp.float32), axis=1)

    came, kept = lax.optimization_barrier((came, kept))
    total = kept + came.astype(jnp.float32)
    rows_left //= 2
    sent = total[rows_left:].astype(jnp.bfloat16)
    kept = total[:rows_left]
    came = lax.ppermute(sent, CUBE, stage_pairs(1))
    came, _ = lax.optimization_barrier((came, row_score))
    spread = (kept + came.astype(jnp.float32)).astype(jnp.bfloat16)
    unit = rows_left // lax.axis_size(REST)
    gathered = lax.all_to_all(
        spread.reshape(-1, unit, half), REST, split_axis=0, concat_axis=0, tiled=True
    ).reshape(-1, 2, unit, half)
    returned_score = send_back(row_score.reshape(expert_count, capacity))
    slot_index = lax.broadcasted_iota(jnp.int32, (expert_count, capacity), 1)
    live_rows = (slot_index < counts[:, None]).astype(jnp.float32)
    route_grad = live_rows * returned_score / route_weight.reshape(expert_count, capacity)

    total = jnp.sum(gathered.astype(jnp.float32), axis=0) / replica_count
    weight_grad = jnp.concatenate([total[0], total[1]], axis=1)[None]
    return (grad_rows, weight_grad, route_grad.reshape(row_total))


def solution(mesh):
    fine = Mesh(mesh.devices.reshape(2, 4, 2, 2, 3, 2, 2, 2), DEVICE)
    in_specs = (P(DEVICE, None), P(DEVICE), P(DEVICE), P(DEVICE, None), P(EXPERT, None, None))
    out_specs = (P(DEVICE, None), P(EXPERT, EDATA, None), P(DEVICE))
    return jax.shard_map(body, mesh=fine, in_specs=in_specs, out_specs=out_specs, check_vma=False)
```

```python
import jax
import jax.numpy as jnp
from jax import lax
from jax.experimental import pallas as pl
from jax.experimental.pallas import tpu as pltpu
from jax.sharding import Mesh, PartitionSpec as P

EXPERT = ("yh", "x")
EDATA = ("y1", "y0", "zc", "z1", "z0", "core")
DEVICE = EXPERT + EDATA
CUBE = ("y1", "y0", "z1", "z0", "core")
STAGES = (("z0", "y0"), ("y0", "z0"))
REST = ("y1", "zc", "z1", "core")


def swap(value, axis):
    return lax.ppermute(value, axis, [(0, 1), (1, 0)])


def pick(value, index, axis):
    return lax.dynamic_index_in_dim(value, index, axis, keepdims=False)


def send_back(score):
    capacity = score.shape[1]
    score = score.reshape(2, 2, 2, 1, capacity)
    for axis, bit in (("yh", 1), ("x", 2), ("x", 1)):
        mine = lax.axis_index(axis) // bit % 2
        size = lax.axis_size(axis)
        kept = pick(score, mine, 0)
        came = lax.ppermute(pick(score, 1 - mine, 0), axis, [(i, i ^ bit) for i in range(size)])
        both = jnp.where(mine == 0, jnp.stack([kept, came], -2), jnp.stack([came, kept], -2))
        score = both.reshape(kept.shape[:-2] + (-1, capacity))
    return score


def stage_pairs(stage):
    pairs = []
    for source in range(32):
        axis = STAGES[stage][source % 2]
        pairs.append((source, source ^ (16 >> CUBE.index(axis))))
    return pairs


def block_order(cube_count):
    rest = 4 * cube_count
    block = jnp.arange(4 * rest, dtype=jnp.int32)
    place_y1, place_cube, place_z1 = block % rest // (rest // 2), block % (rest // 2) // 2, block % 2
    orders = []
    for core in range(2):
        place = {}
        for stage in range(2):
            axis = STAGES[stage][core]
            place[axis] = lax.axis_index(axis) ^ (block // rest // (2 >> stage) % 2)
        orders.append(
            (((place_y1 * 2 + place["y0"]) * cube_count + place_cube) * 2 + place_z1) * 2 + place["z0"]
        )
    return jnp.where(lax.axis_index("core") == 0, orders[0], orders[1]).astype(jnp.int32)


def reorder_kernel(order_ref, source_ref, out_ref):
    count = order_ref.shape[0]
    unit = source_ref.shape[0] // count
    for block in range(count):
        start = pl.multiple_of(order_ref[block] * unit, unit)
        out_ref[block * unit : (block + 1) * unit, :] = source_ref[pl.ds(start, unit), :]


def reorder(source, order):
    return pl.pallas_call(
        reorder_kernel,
        out_shape=jax.ShapeDtypeStruct(source.shape, source.dtype),
        in_specs=[pl.BlockSpec(memory_space=pltpu.SMEM), pl.BlockSpec(memory_space=pltpu.VMEM)],
        out_specs=pl.BlockSpec(memory_space=pltpu.VMEM),
        compiler_params=pltpu.CompilerParams(vmem_limit_bytes=16 * 2**20),
        cost_estimate=pl.CostEstimate(flops=0, bytes_accessed=2 * 2 * source.size, transcendentals=0),
    )(order, source)


def scale_kernel(counts_ref, route_ref, grad_ref, out_ref):
    step = pl.program_id(0)
    blocks, _, capacity, half = out_ref.shape
    slots = route_ref.shape[1]
    slot = lax.broadcasted_iota(jnp.int32, (capacity, slots), 1)
    row = lax.broadcasted_iota(jnp.int32, (capacity, slots), 0)
    for block in range(blocks):
        expert = step * blocks + block
        own = (slot == row + expert * capacity) & (row < counts_ref[expert])
        slot_weight = jnp.sum(jnp.where(own, route_ref[...], 0.0), axis=1, keepdims=True)
        rows = grad_ref[block * capacity : (block + 1) * capacity, :].astype(jnp.float32) * slot_weight
        rows = rows.astype(jnp.bfloat16)
        out_ref[block, 0] = rows[:, :half]
        out_ref[block, 1] = rows[:, half:]


def scale(counts, route_weight, grad_out):
    row_total, feature_count = grad_out.shape
    expert_count = counts.shape[0]
    capacity = row_total // expert_count
    half = feature_count // 2
    blocks = 2
    return pl.pallas_call(
        scale_kernel,
        grid=(expert_count // blocks,),
        out_shape=jax.ShapeDtypeStruct((expert_count, 2, capacity, half), jnp.bfloat16),
        in_specs=[
            pl.BlockSpec(memory_space=pltpu.SMEM),
            pl.BlockSpec((1, row_total), lambda step: (0, 0)),
            pl.BlockSpec((blocks * capacity, feature_count), lambda step: (step, 0)),
        ],
        out_specs=pl.BlockSpec((blocks, 2, capacity, half), lambda step: (step, 0, 0, 0)),
        compiler_params=pltpu.CompilerParams(vmem_limit_bytes=60 * 2**20),
        cost_estimate=pl.CostEstimate(
            flops=grad_out.size, bytes_accessed=4 * grad_out.size, transcendentals=0
        ),
    )(counts, route_weight.reshape(1, row_total), grad_out)


def body(grad_out, route_weight, counts, preact, down_weight):
    row_total, feature_count = grad_out.shape
    expert_count = lax.axis_size(EXPERT)
    capacity = row_total // expert_count
    hidden_count = down_weight.shape[1]
    half = feature_count // 2
    replica_count = lax.axis_size(EDATA)
    core = lax.axis_index("core")
    cube_count = lax.axis_size("zc")

    outgoing = scale(counts, route_weight, grad_out)
    arrived = lax.all_to_all(
        outgoing.reshape(expert_count * 2, capacity, half),
        EXPERT + ("core",), split_axis=0, concat_axis=0, tiled=True,
    ).reshape(expert_count, 2, capacity, half)

    gate_value = preact[:, :hidden_count].astype(jnp.float32)
    up_value = preact[:, hidden_count:].astype(jnp.float32)
    sigmoid_gate = jax.nn.sigmoid(gate_value)
    silu_gate = gate_value * sigmoid_gate
    hidden_act = (silu_gate * up_value).astype(jnp.bfloat16)
    hidden_blocks = hidden_act.reshape(expert_count, capacity, hidden_count)
    other_blocks = swap(hidden_blocks, "core")
    first_core = core == 0
    hidden_all = jnp.stack(
        [
            jnp.where(first_core, hidden_blocks, other_blocks),
            jnp.where(first_core, other_blocks, hidden_blocks),
        ],
        axis=1,
    ).reshape(2 * row_total, hidden_count)
    hidden_units = reorder(hidden_all.T, block_order(cube_count))

    def product(units, rows):
        return lax.dot_general(
            units, rows.reshape(2 * row_total, half), (((1,), (0,)), ((), ())),
            preferred_element_type=jnp.float32,
        )

    quarter = hidden_count // 4
    sent_first = product(hidden_units[3 * quarter :], arrived).astype(jnp.bfloat16)
    came_first = lax.ppermute(sent_first, CUBE, stage_pairs(0))
    arrived, _ = lax.optimization_barrier((arrived, sent_first))
    sent_second = product(hidden_units[2 * quarter : 3 * quarter], arrived).astype(jnp.bfloat16)
    came_second = lax.ppermute(sent_second, CUBE, stage_pairs(0))
    arrived, _ = lax.optimization_barrier((arrived, sent_second))
    kept = product(hidden_units[: 2 * quarter], arrived)
    came_first, kept = lax.optimization_barrier((came_first, kept))
    passed = (kept[quarter:] + came_first.astype(jnp.float32)).astype(jnp.bfloat16)
    came = lax.ppermute(passed, CUBE, stage_pairs(1))
    arrived, _ = lax.optimization_barrier((arrived, passed))

    weight_half = lax.dynamic_slice(
        down_weight[0], (0, core * half), (hidden_count, half)
    )
    grad_partial = lax.dot_general(
        arrived.reshape(2 * row_total, half), weight_half, (((1,), (1,)), ((), ())),
        preferred_element_type=jnp.float32,
    ).reshape(expert_count, 2, capacity, hidden_count)
    grad_other = swap(pick(grad_partial, 1 - core, 1), "core")
    grad_hidden = (pick(grad_partial, core, 1) + grad_other).reshape(row_total, hidden_count)
    grad_gate = grad_hidden * up_value * sigmoid_gate * (1.0 + gate_value * (1.0 - sigmoid_gate))
    grad_up = grad_hidden * silu_gate
    grad_rows = jnp.concatenate([grad_gate, grad_up], axis=1).astype(jnp.bfloat16)
    row_score = jnp.sum(grad_hidden * hidden_act.astype(jnp.float32), axis=1)

    spread = (
        kept[:quarter] + came_second.astype(jnp.float32) + came.astype(jnp.float32)
    ).astype(jnp.bfloat16)
    unit = quarter // lax.axis_size(REST)
    gathered = lax.all_to_all(
        spread.reshape(-1, unit, half), REST, split_axis=0, concat_axis=0, tiled=True
    ).reshape(-1, 2, unit, half)
    returned_score = send_back(row_score.reshape(expert_count, capacity))
    slot_index = lax.broadcasted_iota(jnp.int32, (expert_count, capacity), 1)
    live_rows = (slot_index < counts[:, None]).astype(jnp.float32)
    route_grad = live_rows * returned_score / route_weight.reshape(expert_count, capacity)

    total = jnp.sum(gathered.astype(jnp.float32), axis=0) / replica_count
    weight_grad = jnp.concatenate([total[0], total[1]], axis=1)[None]
    return (grad_rows, weight_grad, route_grad.reshape(row_total))


def solution(mesh):
    fine = Mesh(mesh.devices.reshape(2, 4, 2, 2, 3, 2, 2, 2), DEVICE)
    in_specs = (P(DEVICE, None), P(DEVICE), P(DEVICE), P(DEVICE, None), P(EXPERT, None, None))
    out_specs = (P(DEVICE, None), P(EXPERT, EDATA, None), P(DEVICE))
    return jax.shard_map(body, mesh=fine, in_specs=in_specs, out_specs=out_specs, check_vma=False)
```

```python
import jax
import jax.numpy as jnp
from jax import lax
from jax.experimental import pallas as pl
from jax.experimental.pallas import tpu as pltpu
from jax.sharding import Mesh, PartitionSpec as P

EXPERT = ("yh", "x")
EDATA = ("y1", "y0", "zc", "z1", "z0", "core")
DEVICE = EXPERT + EDATA
CUBE = ("y1", "y0", "z1", "z0", "core")
STAGES = (("z0", "y0"), ("y0", "z0"))
REST = ("y1", "zc", "z1", "core")


def swap(value, axis):
    return lax.ppermute(value, axis, [(0, 1), (1, 0)])


def pick(value, index, axis):
    return lax.dynamic_index_in_dim(value, index, axis, keepdims=False)


def send_back(score):
    capacity = score.shape[1]
    width = lax.axis_size("x")
    score = score.reshape(2, width, capacity)
    half, place = lax.axis_index("yh"), lax.axis_index("x")
    kept = pick(score, half, 0)
    came = swap(pick(score, 1 - half, 0), "yh")
    score = jnp.where(half == 0, jnp.stack([kept, came], 1), jnp.stack([came, kept], 1))
    source = lax.broadcasted_iota(jnp.int32, (2, width, capacity), 1)
    returned = jnp.zeros((2, width, capacity), jnp.float32)
    for shift in range(width):
        part = pick(score, (place + shift) % width, 0)
        if shift > 0:
            part = lax.ppermute(part, "x", [(i, (i + shift) % width) for i in range(width)])
        returned = jnp.where(source == (place + width - shift) % width, part[:, None], returned)
    return returned.reshape(2 * width, capacity)


def stage_pairs(stage):
    pairs = []
    for source in range(32):
        axis = STAGES[stage][source % 2]
        pairs.append((source, source ^ (16 >> CUBE.index(axis))))
    return pairs


def block_order(cube_count):
    rest = 4 * cube_count
    block = jnp.arange(4 * rest, dtype=jnp.int32)
    place_y1, place_cube, place_z1 = block % rest // (rest // 2), block % (rest // 2) // 2, block % 2
    orders = []
    for core in range(2):
        place = {}
        for stage in range(2):
            axis = STAGES[stage][core]
            place[axis] = lax.axis_index(axis) ^ (block // rest // (2 >> stage) % 2)
        orders.append(
            (((place_y1 * 2 + place["y0"]) * cube_count + place_cube) * 2 + place_z1) * 2 + place["z0"]
        )
    return jnp.where(lax.axis_index("core") == 0, orders[0], orders[1]).astype(jnp.int32)


def reorder_kernel(order_ref, source_ref, out_ref):
    count = order_ref.shape[0]
    unit = source_ref.shape[0] // count
    for block in range(count):
        start = pl.multiple_of(order_ref[block] * unit, unit)
        out_ref[block * unit : (block + 1) * unit, :] = source_ref[pl.ds(start, unit), :]


def reorder(source, order):
    return pl.pallas_call(
        reorder_kernel,
        out_shape=jax.ShapeDtypeStruct(source.shape, source.dtype),
        in_specs=[pl.BlockSpec(memory_space=pltpu.SMEM), pl.BlockSpec(memory_space=pltpu.VMEM)],
        out_specs=pl.BlockSpec(memory_space=pltpu.VMEM),
        compiler_params=pltpu.CompilerParams(vmem_limit_bytes=16 * 2**20),
        cost_estimate=pl.CostEstimate(flops=0, bytes_accessed=2 * 2 * source.size, transcendentals=0),
    )(order, source)


def scale_kernel(counts_ref, route_ref, grad_ref, out_ref):
    step = pl.program_id(0)
    blocks, _, capacity, half = out_ref.shape
    slots = route_ref.shape[1]
    slot = lax.broadcasted_iota(jnp.int32, (capacity, slots), 1)
    row = lax.broadcasted_iota(jnp.int32, (capacity, slots), 0)
    for block in range(blocks):
        expert = step * blocks + block
        own = (slot == row + expert * capacity) & (row < counts_ref[expert])
        slot_weight = jnp.sum(jnp.where(own, route_ref[...], 0.0), axis=1, keepdims=True)
        rows = grad_ref[block * capacity : (block + 1) * capacity, :].astype(jnp.float32) * slot_weight
        rows = rows.astype(jnp.bfloat16)
        out_ref[block, 0] = rows[:, :half]
        out_ref[block, 1] = rows[:, half:]


def scale(counts, route_weight, grad_out):
    row_total, feature_count = grad_out.shape
    expert_count = counts.shape[0]
    capacity = row_total // expert_count
    half = feature_count // 2
    blocks = 2
    return pl.pallas_call(
        scale_kernel,
        grid=(expert_count // blocks,),
        out_shape=jax.ShapeDtypeStruct((expert_count, 2, capacity, half), jnp.bfloat16),
        in_specs=[
            pl.BlockSpec(memory_space=pltpu.SMEM),
            pl.BlockSpec((1, row_total), lambda step: (0, 0)),
            pl.BlockSpec((blocks * capacity, feature_count), lambda step: (step, 0)),
        ],
        out_specs=pl.BlockSpec((blocks, 2, capacity, half), lambda step: (step, 0, 0, 0)),
        compiler_params=pltpu.CompilerParams(vmem_limit_bytes=60 * 2**20),
        cost_estimate=pl.CostEstimate(
            flops=grad_out.size, bytes_accessed=4 * grad_out.size, transcendentals=0
        ),
    )(counts, route_weight.reshape(1, row_total), grad_out)


def body(grad_out, route_weight, counts, preact, down_weight):
    row_total, feature_count = grad_out.shape
    expert_count = lax.axis_size(EXPERT)
    capacity = row_total // expert_count
    hidden_count = down_weight.shape[1]
    half = feature_count // 2
    replica_count = lax.axis_size(EDATA)
    core = lax.axis_index("core")
    cube_count = lax.axis_size("zc")

    outgoing = scale(counts, route_weight, grad_out)
    arrived = lax.all_to_all(
        outgoing.reshape(expert_count * 2, capacity, half),
        EXPERT + ("core",), split_axis=0, concat_axis=0, tiled=True,
    ).reshape(expert_count, 2, capacity, half)

    gate_value = preact[:, :hidden_count].astype(jnp.float32)
    up_value = preact[:, hidden_count:].astype(jnp.float32)
    sigmoid_gate = jax.nn.sigmoid(gate_value)
    silu_gate = gate_value * sigmoid_gate
    hidden_act = (silu_gate * up_value).astype(jnp.bfloat16)
    hidden_blocks = hidden_act.reshape(expert_count, capacity, hidden_count)
    other_blocks = swap(hidden_blocks, "core")
    first_core = core == 0
    hidden_all = jnp.stack(
        [
            jnp.where(first_core, hidden_blocks, other_blocks),
            jnp.where(first_core, other_blocks, hidden_blocks),
        ],
        axis=1,
    ).reshape(2 * row_total, hidden_count)
    hidden_units = reorder(hidden_all.T, block_order(cube_count))

    def product(units, rows):
        return lax.dot_general(
            units, rows.reshape(2 * row_total, half), (((1,), (0,)), ((), ())),
            preferred_element_type=jnp.float32,
        )

    quarter = hidden_count // 4
    sent_first = product(hidden_units[3 * quarter :], arrived).astype(jnp.bfloat16)
    came_first = lax.ppermute(sent_first, CUBE, stage_pairs(0))
    arrived, _ = lax.optimization_barrier((arrived, sent_first))
    weight_half = lax.dynamic_slice(
        down_weight[0], (0, core * half), (hidden_count, half)
    )
    grad_partial = lax.dot_general(
        arrived.reshape(2 * row_total, half), weight_half, (((1,), (1,)), ((), ())),
        preferred_element_type=jnp.float32,
    ).reshape(expert_count, 2, capacity, hidden_count)
    arrived, _ = lax.optimization_barrier((arrived, grad_partial))
    sent_second = product(hidden_units[2 * quarter : 3 * quarter], arrived).astype(jnp.bfloat16)
    came_second = lax.ppermute(sent_second, CUBE, stage_pairs(0))
    arrived, _ = lax.optimization_barrier((arrived, sent_second))
    kept = product(hidden_units[: 2 * quarter], arrived)
    came_first, kept = lax.optimization_barrier((came_first, kept))
    passed = (kept[quarter:] + came_first.astype(jnp.float32)).astype(jnp.bfloat16)
    came = lax.ppermute(passed, CUBE, stage_pairs(1))

    grad_other = swap(pick(grad_partial, 1 - core, 1), "core")
    grad_hidden = (pick(grad_partial, core, 1) + grad_other).reshape(row_total, hidden_count)
    grad_gate = grad_hidden * up_value * sigmoid_gate * (1.0 + gate_value * (1.0 - sigmoid_gate))
    grad_up = grad_hidden * silu_gate
    grad_rows = jnp.concatenate([grad_gate, grad_up], axis=1).astype(jnp.bfloat16)
    row_score = jnp.sum(grad_hidden * hidden_act.astype(jnp.float32), axis=1)

    came_second, _ = lax.optimization_barrier((came_second, row_score))
    spread = (
        kept[:quarter] + came_second.astype(jnp.float32) + came.astype(jnp.float32)
    ).astype(jnp.bfloat16)
    unit = quarter // lax.axis_size(REST)
    gathered = lax.all_to_all(
        spread.reshape(-1, unit, half), REST, split_axis=0, concat_axis=0, tiled=True
    ).reshape(-1, 2, unit, half)
    returned_score = send_back(row_score.reshape(expert_count, capacity))
    slot_index = lax.broadcasted_iota(jnp.int32, (expert_count, capacity), 1)
    live_rows = (slot_index < counts[:, None]).astype(jnp.float32)
    route_grad = live_rows * returned_score / route_weight.reshape(expert_count, capacity)

    total = jnp.sum(gathered.astype(jnp.float32), axis=0) / replica_count
    weight_grad = jnp.concatenate([total[0], total[1]], axis=1)[None]
    return (grad_rows, weight_grad, route_grad.reshape(row_total))


def solution(mesh):
    fine = Mesh(mesh.devices.reshape(2, 4, 2, 2, 3, 2, 2, 2), DEVICE)
    in_specs = (P(DEVICE, None), P(DEVICE), P(DEVICE), P(DEVICE, None), P(EXPERT, None, None))
    out_specs = (P(DEVICE, None), P(EXPERT, EDATA, None), P(DEVICE))
    return jax.shard_map(body, mesh=fine, in_specs=in_specs, out_specs=out_specs, check_vma=False)
```

```python
import jax
import jax.numpy as jnp
from jax import lax
from jax.experimental import pallas as pl
from jax.experimental.pallas import tpu as pltpu
from jax.sharding import Mesh, PartitionSpec as P

EXPERT = ("yh", "x")
EDATA = ("y1", "y0", "zc", "z1", "z0", "core")
DEVICE = EXPERT + EDATA
CUBE = ("y1", "y0", "z1", "z0", "core")
STAGES = (("z0", "y0"), ("y0", "z0"))
REST = ("y1", "zc", "z1", "core")


def swap(value, axis):
    return lax.ppermute(value, axis, [(0, 1), (1, 0)])


def pick(value, index, axis):
    return lax.dynamic_index_in_dim(value, index, axis, keepdims=False)


def send_back(score):
    capacity = score.shape[1]
    width = lax.axis_size("x")
    score = score.reshape(2, width, capacity)
    half, place = lax.axis_index("yh"), lax.axis_index("x")
    kept = pick(score, half, 0)
    came = swap(pick(score, 1 - half, 0), "yh")
    score = jnp.where(half == 0, jnp.stack([kept, came], 1), jnp.stack([came, kept], 1))
    parts = []
    for shift in range(width):
        part = pick(score, (place + shift) % width, 0)
        if shift > 0:
            part = lax.ppermute(part, "x", [(i, (i + shift) % width) for i in range(width)])
        parts.append(part)
    turned = jnp.stack([parts[-k % width] for k in range(width)] * 2, axis=1)
    returned = lax.dynamic_slice_in_dim(turned, (width - place) % width, width, axis=1)
    return returned.reshape(2 * width, capacity)


def stage_pairs(stage):
    pairs = []
    for source in range(32):
        axis = STAGES[stage][source % 2]
        pairs.append((source, source ^ (16 >> CUBE.index(axis))))
    return pairs


def block_order(cube_count):
    rest = 4 * cube_count
    block = jnp.arange(4 * rest, dtype=jnp.int32)
    place_y1, place_cube, place_z1 = block % rest // (rest // 2), block % (rest // 2) // 2, block % 2
    orders = []
    for core in range(2):
        place = {}
        for stage in range(2):
            axis = STAGES[stage][core]
            place[axis] = lax.axis_index(axis) ^ (block // rest // (2 >> stage) % 2)
        orders.append(
            (((place_y1 * 2 + place["y0"]) * cube_count + place_cube) * 2 + place_z1) * 2 + place["z0"]
        )
    return jnp.where(lax.axis_index("core") == 0, orders[0], orders[1]).astype(jnp.int32)


def reorder_kernel(order_ref, source_ref, out_ref):
    count = order_ref.shape[0]
    unit = source_ref.shape[0] // count
    for block in range(count):
        start = pl.multiple_of(order_ref[block] * unit, unit)
        out_ref[block * unit : (block + 1) * unit, :] = source_ref[pl.ds(start, unit), :]


def reorder(source, order):
    return pl.pallas_call(
        reorder_kernel,
        out_shape=jax.ShapeDtypeStruct(source.shape, source.dtype),
        in_specs=[pl.BlockSpec(memory_space=pltpu.SMEM), pl.BlockSpec(memory_space=pltpu.VMEM)],
        out_specs=pl.BlockSpec(memory_space=pltpu.VMEM),
        compiler_params=pltpu.CompilerParams(vmem_limit_bytes=16 * 2**20),
        cost_estimate=pl.CostEstimate(flops=0, bytes_accessed=2 * 2 * source.size, transcendentals=0),
    )(order, source)


def scale_kernel(counts_ref, route_ref, grad_ref, out_ref):
    step = pl.program_id(0)
    blocks, _, capacity, half = out_ref.shape
    slots = route_ref.shape[1]
    slot = lax.broadcasted_iota(jnp.int32, (capacity, slots), 1)
    row = lax.broadcasted_iota(jnp.int32, (capacity, slots), 0)
    for block in range(blocks):
        expert = step * blocks + block
        own = (slot == row + expert * capacity) & (row < counts_ref[expert])
        slot_weight = jnp.sum(jnp.where(own, route_ref[...], 0.0), axis=1, keepdims=True)
        rows = grad_ref[block * capacity : (block + 1) * capacity, :].astype(jnp.float32) * slot_weight
        rows = rows.astype(jnp.bfloat16)
        out_ref[block, 0] = rows[:, :half]
        out_ref[block, 1] = rows[:, half:]


def scale(counts, route_weight, grad_out):
    row_total, feature_count = grad_out.shape
    expert_count = counts.shape[0]
    capacity = row_total // expert_count
    half = feature_count // 2
    blocks = expert_count // 2
    return pl.pallas_call(
        scale_kernel,
        grid=(expert_count // blocks,),
        out_shape=jax.ShapeDtypeStruct((expert_count, 2, capacity, half), jnp.bfloat16),
        in_specs=[
            pl.BlockSpec(memory_space=pltpu.SMEM),
            pl.BlockSpec((1, row_total), lambda step: (0, 0)),
            pl.BlockSpec((blocks * capacity, feature_count), lambda step: (step, 0)),
        ],
        out_specs=pl.BlockSpec((blocks, 2, capacity, half), lambda step: (step, 0, 0, 0)),
        compiler_params=pltpu.CompilerParams(vmem_limit_bytes=60 * 2**20),
        cost_estimate=pl.CostEstimate(
            flops=grad_out.size, bytes_accessed=4 * grad_out.size, transcendentals=0
        ),
    )(counts, route_weight.reshape(1, row_total), grad_out)


def body(grad_out, route_weight, counts, preact, down_weight):
    row_total, feature_count = grad_out.shape
    expert_count = lax.axis_size(EXPERT)
    capacity = row_total // expert_count
    hidden_count = down_weight.shape[1]
    half = feature_count // 2
    replica_count = lax.axis_size(EDATA)
    core = lax.axis_index("core")
    cube_count = lax.axis_size("zc")

    outgoing = scale(counts, route_weight, grad_out)
    arrived = lax.all_to_all(
        outgoing.reshape(expert_count * 2, capacity, half),
        EXPERT + ("core",), split_axis=0, concat_axis=0, tiled=True,
    ).reshape(expert_count, 2, capacity, half)

    gate_value = preact[:, :hidden_count].astype(jnp.float32)
    up_value = preact[:, hidden_count:].astype(jnp.float32)
    sigmoid_gate = jax.nn.sigmoid(gate_value)
    silu_gate = gate_value * sigmoid_gate
    hidden_act = (silu_gate * up_value).astype(jnp.bfloat16)
    hidden_blocks = hidden_act.reshape(expert_count, capacity, hidden_count)
    other_blocks = swap(hidden_blocks, "core")
    first_core = core == 0
    hidden_all = jnp.stack(
        [
            jnp.where(first_core, hidden_blocks, other_blocks),
            jnp.where(first_core, other_blocks, hidden_blocks),
        ],
        axis=1,
    ).reshape(2 * row_total, hidden_count)
    hidden_units = reorder(hidden_all.T, block_order(cube_count))

    def product(units, rows):
        return lax.dot_general(
            units, rows.reshape(2 * row_total, half), (((1,), (0,)), ((), ())),
            preferred_element_type=jnp.float32,
        )

    quarter = hidden_count // 4
    sent_first = product(hidden_units[3 * quarter :], arrived).astype(jnp.bfloat16)
    came_first = lax.ppermute(sent_first, CUBE, stage_pairs(0))
    arrived, _ = lax.optimization_barrier((arrived, sent_first))
    weight_half = lax.dynamic_slice(
        down_weight[0], (0, core * half), (hidden_count, half)
    )
    grad_partial = lax.dot_general(
        arrived.reshape(2 * row_total, half), weight_half, (((1,), (1,)), ((), ())),
        preferred_element_type=jnp.float32,
    ).reshape(expert_count, 2, capacity, hidden_count)
    arrived, _ = lax.optimization_barrier((arrived, grad_partial))
    sent_second = product(hidden_units[2 * quarter : 3 * quarter], arrived).astype(jnp.bfloat16)
    came_second = lax.ppermute(sent_second, CUBE, stage_pairs(0))
    arrived, _ = lax.optimization_barrier((arrived, sent_second))
    kept = product(hidden_units[: 2 * quarter], arrived)
    came_first, kept = lax.optimization_barrier((came_first, kept))
    passed = (kept[quarter:] + came_first.astype(jnp.float32)).astype(jnp.bfloat16)
    came = lax.ppermute(passed, CUBE, stage_pairs(1))
    grad_partial, _ = lax.optimization_barrier((grad_partial, passed))

    grad_other = swap(pick(grad_partial, 1 - core, 1), "core")
    grad_hidden = (pick(grad_partial, core, 1) + grad_other).reshape(row_total, hidden_count)
    grad_gate = grad_hidden * up_value * sigmoid_gate * (1.0 + gate_value * (1.0 - sigmoid_gate))
    grad_up = grad_hidden * silu_gate
    grad_rows = jnp.concatenate([grad_gate, grad_up], axis=1).astype(jnp.bfloat16)
    row_score = jnp.sum(grad_hidden * hidden_act.astype(jnp.float32), axis=1)

    spread = (
        kept[:quarter] + came_second.astype(jnp.float32) + came.astype(jnp.float32)
    ).astype(jnp.bfloat16)
    unit = quarter // lax.axis_size(REST)
    gathered = lax.all_to_all(
        spread.reshape(-1, unit, half), REST, split_axis=0, concat_axis=0, tiled=True
    ).reshape(-1, 2, unit, half)
    returned_score = send_back(row_score.reshape(expert_count, capacity))
    slot_index = lax.broadcasted_iota(jnp.int32, (expert_count, capacity), 1)
    live_rows = (slot_index < counts[:, None]).astype(jnp.float32)
    route_grad = live_rows * returned_score / route_weight.reshape(expert_count, capacity)

    total = jnp.sum(gathered.astype(jnp.float32), axis=0) / replica_count
    weight_grad = jnp.concatenate([total[0], total[1]], axis=1)[None]
    return (grad_rows, weight_grad, route_grad.reshape(row_total))


def solution(mesh):
    fine = Mesh(mesh.devices.reshape(2, 4, 2, 2, 3, 2, 2, 2), DEVICE)
    in_specs = (P(DEVICE, None), P(DEVICE), P(DEVICE), P(DEVICE, None), P(EXPERT, None, None))
    out_specs = (P(DEVICE, None), P(EXPERT, EDATA, None), P(DEVICE))
    return jax.shard_map(body, mesh=fine, in_specs=in_specs, out_specs=out_specs, check_vma=False)
```

```python
import jax
import jax.numpy as jnp
from jax import lax
from jax.experimental import pallas as pl
from jax.experimental.pallas import tpu as pltpu
from jax.sharding import Mesh, PartitionSpec as P

EXPERT = ("yh", "x")
EDATA = ("y1", "y0", "zc", "z1", "z0", "core")
DEVICE = EXPERT + EDATA
CUBE = ("y1", "y0", "z1", "z0", "core")
STAGES = (("z0", "y0"), ("y0", "z0"))
REST = ("y1", "zc", "z1", "core")


def swap(value, axis):
    return lax.ppermute(value, axis, [(0, 1), (1, 0)])


def pick(value, index, axis):
    return lax.dynamic_index_in_dim(value, index, axis, keepdims=False)


def send_back(score):
    capacity = score.shape[1]
    width = lax.axis_size("x")
    score = score.reshape(2, width, capacity)
    half, place = lax.axis_index("yh"), lax.axis_index("x")
    kept = pick(score, half, 0)
    came = swap(pick(score, 1 - half, 0), "yh")
    score = jnp.where(half == 0, jnp.stack([kept, came], 1), jnp.stack([came, kept], 1))
    parts = []
    for shift in range(width):
        part = pick(score, (place + shift) % width, 0)
        if shift > 0:
            part = lax.ppermute(part, "x", [(i, (i + shift) % width) for i in range(width)])
        parts.append(part)
    turned = jnp.stack([parts[-k % width] for k in range(width)] * 2, axis=1)
    returned = lax.dynamic_slice_in_dim(turned, (width - place) % width, width, axis=1)
    return returned.reshape(2 * width, capacity)


def stage_pairs(stage):
    pairs = []
    for source in range(32):
        axis = STAGES[stage][source % 2]
        pairs.append((source, source ^ (16 >> CUBE.index(axis))))
    return pairs


def block_order(cube_count):
    rest = 4 * cube_count
    block = jnp.arange(4 * rest, dtype=jnp.int32)
    place_y1, place_cube, place_z1 = block % rest // (rest // 2), block % (rest // 2) // 2, block % 2
    orders = []
    for core in range(2):
        place = {}
        for stage in range(2):
            axis = STAGES[stage][core]
            place[axis] = lax.axis_index(axis) ^ (block // rest // (2 >> stage) % 2)
        orders.append(
            (((place_y1 * 2 + place["y0"]) * cube_count + place_cube) * 2 + place_z1) * 2 + place["z0"]
        )
    return jnp.where(lax.axis_index("core") == 0, orders[0], orders[1]).astype(jnp.int32)


def reorder_kernel(order_ref, source_ref, out_ref):
    count = order_ref.shape[0]
    unit = source_ref.shape[0] // count
    for block in range(count):
        start = pl.multiple_of(order_ref[block] * unit, unit)
        out_ref[block * unit : (block + 1) * unit, :] = source_ref[pl.ds(start, unit), :]


def reorder(source, order):
    return pl.pallas_call(
        reorder_kernel,
        out_shape=jax.ShapeDtypeStruct(source.shape, source.dtype),
        in_specs=[pl.BlockSpec(memory_space=pltpu.SMEM), pl.BlockSpec(memory_space=pltpu.VMEM)],
        out_specs=pl.BlockSpec(memory_space=pltpu.VMEM),
        compiler_params=pltpu.CompilerParams(vmem_limit_bytes=16 * 2**20),
        cost_estimate=pl.CostEstimate(flops=0, bytes_accessed=2 * 2 * source.size, transcendentals=0),
    )(order, source)


def scale_kernel(counts_ref, route_ref, grad_ref, out_ref):
    step = pl.program_id(0)
    blocks, _, capacity, half = out_ref.shape
    slots = route_ref.shape[1]
    slot = lax.broadcasted_iota(jnp.int32, (capacity, slots), 1)
    row = lax.broadcasted_iota(jnp.int32, (capacity, slots), 0)
    for block in range(blocks):
        expert = step * blocks + block
        own = (slot == row + expert * capacity) & (row < counts_ref[expert])
        slot_weight = jnp.sum(jnp.where(own, route_ref[...], 0.0), axis=1, keepdims=True)
        rows = grad_ref[block * capacity : (block + 1) * capacity, :].astype(jnp.float32) * slot_weight
        rows = rows.astype(jnp.bfloat16)
        out_ref[block, 0] = rows[:, :half]
        out_ref[block, 1] = rows[:, half:]


def scale(counts, route_weight, grad_out):
    row_total, feature_count = grad_out.shape
    expert_count = counts.shape[0]
    capacity = row_total // expert_count
    half = feature_count // 2
    blocks = expert_count // 2
    return pl.pallas_call(
        scale_kernel,
        grid=(expert_count // blocks,),
        out_shape=jax.ShapeDtypeStruct((expert_count, 2, capacity, half), jnp.bfloat16),
        in_specs=[
            pl.BlockSpec(memory_space=pltpu.SMEM),
            pl.BlockSpec((1, row_total), lambda step: (0, 0)),
            pl.BlockSpec((blocks * capacity, feature_count), lambda step: (step, 0)),
        ],
        out_specs=pl.BlockSpec((blocks, 2, capacity, half), lambda step: (step, 0, 0, 0)),
        compiler_params=pltpu.CompilerParams(vmem_limit_bytes=60 * 2**20),
        cost_estimate=pl.CostEstimate(
            flops=grad_out.size, bytes_accessed=4 * grad_out.size, transcendentals=0
        ),
    )(counts, route_weight.reshape(1, row_total), grad_out)


def body(grad_out, route_weight, counts, preact, down_weight):
    row_total, feature_count = grad_out.shape
    expert_count = lax.axis_size(EXPERT)
    capacity = row_total // expert_count
    hidden_count = down_weight.shape[1]
    half = feature_count // 2
    replica_count = lax.axis_size(EDATA)
    core = lax.axis_index("core")
    cube_count = lax.axis_size("zc")

    outgoing = scale(counts, route_weight, grad_out)
    arrived = lax.all_to_all(
        outgoing.reshape(expert_count * 2, capacity, half),
        EXPERT + ("core",), split_axis=0, concat_axis=0, tiled=True,
    ).reshape(expert_count, 2, capacity, half)

    gate_value = preact[:, :hidden_count].astype(jnp.float32)
    up_value = preact[:, hidden_count:].astype(jnp.float32)
    sigmoid_gate = jax.nn.sigmoid(gate_value)
    silu_gate = gate_value * sigmoid_gate
    hidden_act = (silu_gate * up_value).astype(jnp.bfloat16)
    hidden_blocks = hidden_act.reshape(expert_count, capacity, hidden_count)
    other_blocks = swap(hidden_blocks, "core")
    first_core = core == 0
    hidden_all = jnp.stack(
        [
            jnp.where(first_core, hidden_blocks, other_blocks),
            jnp.where(first_core, other_blocks, hidden_blocks),
        ],
        axis=1,
    ).reshape(2 * row_total, hidden_count)
    hidden_units = reorder(hidden_all.T, block_order(cube_count))

    def product(units, rows):
        return lax.dot_general(
            units, rows.reshape(2 * row_total, half), (((1,), (0,)), ((), ())),
            preferred_element_type=jnp.float32,
        )

    quarter = hidden_count // 4
    sent_first = product(hidden_units[3 * quarter :], arrived).astype(jnp.bfloat16)
    came_first = lax.ppermute(sent_first, CUBE, stage_pairs(0))
    arrived, _ = lax.optimization_barrier((arrived, sent_first))
    weight_half = lax.dynamic_slice(
        down_weight[0], (0, core * half), (hidden_count, half)
    )
    grad_partial = lax.dot_general(
        arrived.reshape(2 * row_total, half), weight_half, (((1,), (1,)), ((), ())),
        preferred_element_type=jnp.float32,
    ).reshape(expert_count, 2, capacity, hidden_count)
    arrived, _ = lax.optimization_barrier((arrived, grad_partial))
    sent_second = product(hidden_units[2 * quarter : 3 * quarter], arrived).astype(jnp.bfloat16)
    came_second = lax.ppermute(sent_second, CUBE, stage_pairs(0))
    arrived, _ = lax.optimization_barrier((arrived, sent_second))
    kept = product(hidden_units[: 2 * quarter], arrived)
    came_first, kept = lax.optimization_barrier((came_first, kept))
    passed = (kept[quarter:] + came_first.astype(jnp.float32)).astype(jnp.bfloat16)
    came = lax.ppermute(passed, CUBE, stage_pairs(1))

    grad_other = swap(pick(grad_partial, 1 - core, 1), "core")
    grad_hidden = (pick(grad_partial, core, 1) + grad_other).reshape(row_total, hidden_count)
    grad_gate = grad_hidden * up_value * sigmoid_gate * (1.0 + gate_value * (1.0 - sigmoid_gate))
    grad_up = grad_hidden * silu_gate
    grad_rows = jnp.concatenate([grad_gate, grad_up], axis=1).astype(jnp.bfloat16)
    row_score = jnp.sum(grad_hidden * hidden_act.astype(jnp.float32), axis=1)

    came_second, _ = lax.optimization_barrier((came_second, row_score))
    spread = (
        kept[:quarter] + came_second.astype(jnp.float32) + came.astype(jnp.float32)
    ).astype(jnp.bfloat16)
    unit = quarter // lax.axis_size(REST)
    gathered = lax.all_to_all(
        spread.reshape(-1, unit, half), REST, split_axis=0, concat_axis=0, tiled=True
    ).reshape(-1, 2, unit, half)
    returned_score = send_back(row_score.reshape(expert_count, capacity))
    slot_index = lax.broadcasted_iota(jnp.int32, (expert_count, capacity), 1)
    live_rows = (slot_index < counts[:, None]).astype(jnp.float32)
    route_grad = live_rows * returned_score / route_weight.reshape(expert_count, capacity)

    total = jnp.sum(gathered.astype(jnp.float32), axis=0) / replica_count
    weight_grad = jnp.concatenate([total[0], total[1]], axis=1)[None]
    return (grad_rows, weight_grad, route_grad.reshape(row_total))


def solution(mesh):
    fine = Mesh(mesh.devices.reshape(2, 4, 2, 2, 3, 2, 2, 2), DEVICE)
    in_specs = (P(DEVICE, None), P(DEVICE), P(DEVICE), P(DEVICE, None), P(EXPERT, None, None))
    out_specs = (P(DEVICE, None), P(EXPERT, EDATA, None), P(DEVICE))
    return jax.shard_map(body, mesh=fine, in_specs=in_specs, out_specs=out_specs, check_vma=False)
```

```python
import jax
import jax.numpy as jnp
from jax import lax
from jax.experimental import pallas as pl
from jax.experimental.pallas import tpu as pltpu
from jax.sharding import Mesh, PartitionSpec as P

EXPERT = ("yh", "x")
EDATA = ("y1", "y0", "zc", "z1", "z0", "core")
DEVICE = EXPERT + EDATA
CUBE = ("y1", "y0", "z1", "z0", "core")
STAGES = (("z0", "y0"), ("y0", "z0"))
REST = ("y1", "zc", "z1", "core")


def swap(value, axis):
    return lax.ppermute(value, axis, [(0, 1), (1, 0)])


def pick(value, index, axis):
    return lax.dynamic_index_in_dim(value, index, axis, keepdims=False)


def send_back(score):
    capacity = score.shape[1]
    width = lax.axis_size("x")
    score = score.reshape(2, width, capacity)
    half, place = lax.axis_index("yh"), lax.axis_index("x")
    kept = pick(score, half, 0)
    came = swap(pick(score, 1 - half, 0), "yh")
    score = jnp.where(half == 0, jnp.stack([kept, came], 1), jnp.stack([came, kept], 1))
    source = lax.broadcasted_iota(jnp.int32, (2, width, capacity), 1)
    returned = jnp.zeros((2, width, capacity), jnp.float32)
    for shift in range(width):
        part = pick(score, (place + shift) % width, 0)
        if shift > 0:
            part = lax.ppermute(part, "x", [(i, (i + shift) % width) for i in range(width)])
        returned = jnp.where(source == (place + width - shift) % width, part[:, None], returned)
    return returned.reshape(2 * width, capacity)


def stage_pairs(stage):
    pairs = []
    for source in range(32):
        axis = STAGES[stage][source % 2]
        pairs.append((source, source ^ (16 >> CUBE.index(axis))))
    return pairs


def block_order(cube_count):
    rest = 4 * cube_count
    block = jnp.arange(4 * rest, dtype=jnp.int32)
    place_y1, place_cube, place_z1 = block % rest // (rest // 2), block % (rest // 2) // 2, block % 2
    orders = []
    for core in range(2):
        place = {}
        for stage in range(2):
            axis = STAGES[stage][core]
            place[axis] = lax.axis_index(axis) ^ (block // rest // (2 >> stage) % 2)
        orders.append(
            (((place_y1 * 2 + place["y0"]) * cube_count + place_cube) * 2 + place_z1) * 2 + place["z0"]
        )
    return jnp.where(lax.axis_index("core") == 0, orders[0], orders[1]).astype(jnp.int32)


def reorder_kernel(order_ref, source_ref, out_ref):
    count = order_ref.shape[0]
    unit = source_ref.shape[0] // count
    for block in range(count):
        start = pl.multiple_of(order_ref[block] * unit, unit)
        out_ref[block * unit : (block + 1) * unit, :] = source_ref[pl.ds(start, unit), :]


def reorder(source, order):
    return pl.pallas_call(
        reorder_kernel,
        out_shape=jax.ShapeDtypeStruct(source.shape, source.dtype),
        in_specs=[pl.BlockSpec(memory_space=pltpu.SMEM), pl.BlockSpec(memory_space=pltpu.VMEM)],
        out_specs=pl.BlockSpec(memory_space=pltpu.VMEM),
        compiler_params=pltpu.CompilerParams(vmem_limit_bytes=16 * 2**20),
        cost_estimate=pl.CostEstimate(flops=0, bytes_accessed=2 * 2 * source.size, transcendentals=0),
    )(order, source)


def scale_kernel(counts_ref, route_ref, grad_ref, out_ref):
    step = pl.program_id(0)
    blocks, _, capacity, half = out_ref.shape
    slots = route_ref.shape[1]
    slot = lax.broadcasted_iota(jnp.int32, (capacity, slots), 1)
    row = lax.broadcasted_iota(jnp.int32, (capacity, slots), 0)
    for block in range(blocks):
        expert = step * blocks + block
        own = (slot == row + expert * capacity) & (row < counts_ref[expert])
        slot_weight = jnp.sum(jnp.where(own, route_ref[...], 0.0), axis=1, keepdims=True)
        rows = grad_ref[block * capacity : (block + 1) * capacity, :].astype(jnp.float32) * slot_weight
        rows = rows.astype(jnp.bfloat16)
        out_ref[block, 0] = rows[:, :half]
        out_ref[block, 1] = rows[:, half:]


def scale(counts, route_weight, grad_out):
    row_total, feature_count = grad_out.shape
    expert_count = counts.shape[0]
    capacity = row_total // expert_count
    half = feature_count // 2
    blocks = expert_count // 2
    return pl.pallas_call(
        scale_kernel,
        grid=(expert_count // blocks,),
        out_shape=jax.ShapeDtypeStruct((expert_count, 2, capacity, half), jnp.bfloat16),
        in_specs=[
            pl.BlockSpec(memory_space=pltpu.SMEM),
            pl.BlockSpec((1, row_total), lambda step: (0, 0)),
            pl.BlockSpec((blocks * capacity, feature_count), lambda step: (step, 0)),
        ],
        out_specs=pl.BlockSpec((blocks, 2, capacity, half), lambda step: (step, 0, 0, 0)),
        compiler_params=pltpu.CompilerParams(vmem_limit_bytes=60 * 2**20),
        cost_estimate=pl.CostEstimate(
            flops=grad_out.size, bytes_accessed=4 * grad_out.size, transcendentals=0
        ),
    )(counts, route_weight.reshape(1, row_total), grad_out)


def body(grad_out, route_weight, counts, preact, down_weight):
    row_total, feature_count = grad_out.shape
    expert_count = lax.axis_size(EXPERT)
    capacity = row_total // expert_count
    hidden_count = down_weight.shape[1]
    half = feature_count // 2
    replica_count = lax.axis_size(EDATA)
    core = lax.axis_index("core")
    cube_count = lax.axis_size("zc")

    outgoing = scale(counts, route_weight, grad_out)
    arrived = lax.all_to_all(
        outgoing.reshape(expert_count * 2, capacity, half),
        EXPERT + ("core",), split_axis=0, concat_axis=0, tiled=True,
    ).reshape(expert_count, 2, capacity, half)

    gate_value = preact[:, :hidden_count].astype(jnp.float32)
    up_value = preact[:, hidden_count:].astype(jnp.float32)
    sigmoid_gate = jax.nn.sigmoid(gate_value)
    silu_gate = gate_value * sigmoid_gate
    hidden_act = (silu_gate * up_value).astype(jnp.bfloat16)
    hidden_blocks = hidden_act.reshape(expert_count, capacity, hidden_count)
    other_blocks = swap(hidden_blocks, "core")
    first_core = core == 0
    hidden_all = jnp.stack(
        [
            jnp.where(first_core, hidden_blocks, other_blocks),
            jnp.where(first_core, other_blocks, hidden_blocks),
        ],
        axis=1,
    ).reshape(2 * row_total, hidden_count)
    hidden_units = reorder(hidden_all.T, block_order(cube_count))

    def product(units, rows):
        return lax.dot_general(
            units, rows.reshape(2 * row_total, half), (((1,), (0,)), ((), ())),
            preferred_element_type=jnp.float32,
        )

    quarter = hidden_count // 4
    sent_first = product(hidden_units[3 * quarter :], arrived).astype(jnp.bfloat16)
    came_first = lax.ppermute(sent_first, CUBE, stage_pairs(0))
    arrived, _ = lax.optimization_barrier((arrived, sent_first))
    weight_half = lax.dynamic_slice(
        down_weight[0], (0, core * half), (hidden_count, half)
    )
    grad_partial = lax.dot_general(
        arrived.reshape(2 * row_total, half), weight_half, (((1,), (1,)), ((), ())),
        preferred_element_type=jnp.float32,
    ).reshape(expert_count, 2, capacity, hidden_count)
    arrived, _ = lax.optimization_barrier((arrived, grad_partial))
    sent_second = product(hidden_units[2 * quarter : 3 * quarter], arrived).astype(jnp.bfloat16)
    came_second = lax.ppermute(sent_second, CUBE, stage_pairs(0))
    arrived, _ = lax.optimization_barrier((arrived, sent_second))
    kept = product(hidden_units[: 2 * quarter], arrived)
    came_first, kept = lax.optimization_barrier((came_first, kept))
    passed = (kept[quarter:] + came_first.astype(jnp.float32)).astype(jnp.bfloat16)
    came = lax.ppermute(passed, CUBE, stage_pairs(1))

    grad_other = swap(pick(grad_partial, 1 - core, 1), "core")
    grad_hidden = (pick(grad_partial, core, 1) + grad_other).reshape(row_total, hidden_count)
    grad_gate = grad_hidden * up_value * sigmoid_gate * (1.0 + gate_value * (1.0 - sigmoid_gate))
    grad_up = grad_hidden * silu_gate
    grad_rows = jnp.concatenate([grad_gate, grad_up], axis=1).astype(jnp.bfloat16)
    row_score = jnp.sum(grad_hidden * hidden_act.astype(jnp.float32), axis=1)

    came_second, _ = lax.optimization_barrier((came_second, row_score))
    spread = (
        kept[:quarter] + came_second.astype(jnp.float32) + came.astype(jnp.float32)
    ).astype(jnp.bfloat16)
    unit = quarter // lax.axis_size(REST)
    gathered = lax.all_to_all(
        spread.reshape(-1, unit, half), REST, split_axis=0, concat_axis=0, tiled=True
    ).reshape(-1, 2, unit, half)
    returned_score = send_back(row_score.reshape(expert_count, capacity))
    slot_index = lax.broadcasted_iota(jnp.int32, (expert_count, capacity), 1)
    live_rows = (slot_index < counts[:, None]).astype(jnp.float32)
    route_grad = live_rows * returned_score / route_weight.reshape(expert_count, capacity)

    total = jnp.sum(gathered.astype(jnp.float32), axis=0) / replica_count
    weight_grad = jnp.concatenate([total[0], total[1]], axis=1)[None]
    return (grad_rows, weight_grad, route_grad.reshape(row_total))


def solution(mesh):
    fine = Mesh(mesh.devices.reshape(2, 4, 2, 2, 3, 2, 2, 2), DEVICE)
    in_specs = (P(DEVICE, None), P(DEVICE), P(DEVICE), P(DEVICE, None), P(EXPERT, None, None))
    out_specs = (P(DEVICE, None), P(EXPERT, EDATA, None), P(DEVICE))
    return jax.shard_map(body, mesh=fine, in_specs=in_specs, out_specs=out_specs, check_vma=False)
```

```python
import jax
import jax.numpy as jnp
from jax import lax
from jax.experimental import pallas as pl
from jax.experimental.pallas import tpu as pltpu
from jax.sharding import Mesh, PartitionSpec as P

EXPERT = ("yh", "x")
EDATA = ("y1", "y0", "zc", "z1", "z0", "core")
DEVICE = EXPERT + EDATA
CUBE = ("y1", "y0", "z1", "z0", "core")
STAGES = (("z0", "y0"), ("y0", "z0"))
REST = ("y1", "zc", "z1", "core")


def swap(value, axis):
    return lax.ppermute(value, axis, [(0, 1), (1, 0)])


def pick(value, index, axis):
    return lax.dynamic_index_in_dim(value, index, axis, keepdims=False)


def send_back(score, source):
    capacity = score.shape[1]
    width = lax.axis_size("x")
    score = score.reshape(2, width, capacity)
    half, place = lax.axis_index("yh"), lax.axis_index("x")
    kept = pick(score, half, 0)
    came = swap(pick(score, 1 - half, 0), "yh")
    score = jnp.where(half == 0, jnp.stack([kept, came], 1), jnp.stack([came, kept], 1))
    returned = jnp.zeros((2, width, capacity), jnp.float32)
    for shift in range(width):
        part = pick(score, (place + shift) % width, 0)
        if shift > 0:
            part = lax.ppermute(part, "x", [(i, (i + shift) % width) for i in range(width)])
        returned = jnp.where(source == shift, part[:, None], returned)
    return returned.reshape(2 * width, capacity)


def stage_pairs(stage):
    pairs = []
    for source in range(32):
        axis = STAGES[stage][source % 2]
        pairs.append((source, source ^ (16 >> CUBE.index(axis))))
    return pairs


def block_order(cube_count):
    rest = 4 * cube_count
    block = jnp.arange(4 * rest, dtype=jnp.int32)
    place_y1, place_cube, place_z1 = block % rest // (rest // 2), block % (rest // 2) // 2, block % 2
    orders = []
    for core in range(2):
        place = {}
        for stage in range(2):
            axis = STAGES[stage][core]
            place[axis] = lax.axis_index(axis) ^ (block // rest // (2 >> stage) % 2)
        orders.append(
            (((place_y1 * 2 + place["y0"]) * cube_count + place_cube) * 2 + place_z1) * 2 + place["z0"]
        )
    return jnp.where(lax.axis_index("core") == 0, orders[0], orders[1]).astype(jnp.int32)


def reorder_kernel(order_ref, source_ref, out_ref):
    count = order_ref.shape[0]
    unit = source_ref.shape[0] // count
    for block in range(count):
        start = pl.multiple_of(order_ref[block] * unit, unit)
        out_ref[block * unit : (block + 1) * unit, :] = source_ref[pl.ds(start, unit), :]


def reorder(source, order):
    return pl.pallas_call(
        reorder_kernel,
        out_shape=jax.ShapeDtypeStruct(source.shape, source.dtype),
        in_specs=[pl.BlockSpec(memory_space=pltpu.SMEM), pl.BlockSpec(memory_space=pltpu.VMEM)],
        out_specs=pl.BlockSpec(memory_space=pltpu.VMEM),
        compiler_params=pltpu.CompilerParams(vmem_limit_bytes=16 * 2**20),
        cost_estimate=pl.CostEstimate(flops=0, bytes_accessed=2 * 2 * source.size, transcendentals=0),
    )(order, source)


def scale_kernel(counts_ref, route_ref, grad_ref, out_ref):
    step = pl.program_id(0)
    blocks, _, capacity, half = out_ref.shape
    slots = route_ref.shape[1]
    slot = lax.broadcasted_iota(jnp.int32, (capacity, slots), 1)
    row = lax.broadcasted_iota(jnp.int32, (capacity, slots), 0)
    for block in range(blocks):
        expert = step * blocks + block
        own = (slot == row + expert * capacity) & (row < counts_ref[expert])
        slot_weight = jnp.sum(jnp.where(own, route_ref[...], 0.0), axis=1, keepdims=True)
        rows = grad_ref[block * capacity : (block + 1) * capacity, :].astype(jnp.float32) * slot_weight
        rows = rows.astype(jnp.bfloat16)
        out_ref[block, 0] = rows[:, :half]
        out_ref[block, 1] = rows[:, half:]


def scale(counts, route_weight, grad_out):
    row_total, feature_count = grad_out.shape
    expert_count = counts.shape[0]
    capacity = row_total // expert_count
    half = feature_count // 2
    blocks = expert_count // 2
    return pl.pallas_call(
        scale_kernel,
        grid=(expert_count // blocks,),
        out_shape=jax.ShapeDtypeStruct((expert_count, 2, capacity, half), jnp.bfloat16),
        in_specs=[
            pl.BlockSpec(memory_space=pltpu.SMEM),
            pl.BlockSpec((1, row_total), lambda step: (0, 0)),
            pl.BlockSpec((blocks * capacity, feature_count), lambda step: (step, 0)),
        ],
        out_specs=pl.BlockSpec((blocks, 2, capacity, half), lambda step: (step, 0, 0, 0)),
        compiler_params=pltpu.CompilerParams(vmem_limit_bytes=60 * 2**20),
        cost_estimate=pl.CostEstimate(
            flops=grad_out.size, bytes_accessed=4 * grad_out.size, transcendentals=0
        ),
    )(counts, route_weight.reshape(1, row_total), grad_out)


def body(grad_out, route_weight, counts, preact, down_weight):
    row_total, feature_count = grad_out.shape
    expert_count = lax.axis_size(EXPERT)
    capacity = row_total // expert_count
    hidden_count = down_weight.shape[1]
    half = feature_count // 2
    replica_count = lax.axis_size(EDATA)
    core = lax.axis_index("core")
    cube_count = lax.axis_size("zc")

    outgoing = scale(counts, route_weight, grad_out)
    arrived = lax.all_to_all(
        outgoing.reshape(expert_count * 2, capacity, half),
        EXPERT + ("core",), split_axis=0, concat_axis=0, tiled=True,
    ).reshape(expert_count, 2, capacity, half)

    gate_value = preact[:, :hidden_count].astype(jnp.float32)
    up_value = preact[:, hidden_count:].astype(jnp.float32)
    sigmoid_gate = jax.nn.sigmoid(gate_value)
    silu_gate = gate_value * sigmoid_gate
    hidden_act = (silu_gate * up_value).astype(jnp.bfloat16)
    hidden_blocks = hidden_act.reshape(expert_count, capacity, hidden_count)
    other_blocks = swap(hidden_blocks, "core")
    first_core = core == 0
    hidden_all = jnp.stack(
        [
            jnp.where(first_core, hidden_blocks, other_blocks),
            jnp.where(first_core, other_blocks, hidden_blocks),
        ],
        axis=1,
    ).reshape(2 * row_total, hidden_count)
    hidden_units = reorder(hidden_all.T, block_order(cube_count))
    width = lax.axis_size("x")
    source = lax.broadcasted_iota(jnp.int32, (2, width, capacity), 1)
    source = (lax.axis_index("x") + width - source) % width
    hidden_units, source = lax.optimization_barrier((hidden_units, source))

    def product(units, rows):
        return lax.dot_general(
            units, rows.reshape(2 * row_total, half), (((1,), (0,)), ((), ())),
            preferred_element_type=jnp.float32,
        )

    quarter = hidden_count // 4
    sent_first = product(hidden_units[3 * quarter :], arrived).astype(jnp.bfloat16)
    came_first = lax.ppermute(sent_first, CUBE, stage_pairs(0))
    arrived, _ = lax.optimization_barrier((arrived, sent_first))
    weight_half = lax.dynamic_slice(
        down_weight[0], (0, core * half), (hidden_count, half)
    )
    grad_partial = lax.dot_general(
        arrived.reshape(2 * row_total, half), weight_half, (((1,), (1,)), ((), ())),
        preferred_element_type=jnp.float32,
    ).reshape(expert_count, 2, capacity, hidden_count)
    arrived, _ = lax.optimization_barrier((arrived, grad_partial))
    sent_second = product(hidden_units[2 * quarter : 3 * quarter], arrived).astype(jnp.bfloat16)
    came_second = lax.ppermute(sent_second, CUBE, stage_pairs(0))
    arrived, _ = lax.optimization_barrier((arrived, sent_second))
    kept = product(hidden_units[: 2 * quarter], arrived)
    came_first, kept = lax.optimization_barrier((came_first, kept))
    passed = (kept[quarter:] + came_first.astype(jnp.float32)).astype(jnp.bfloat16)
    came = lax.ppermute(passed, CUBE, stage_pairs(1))

    grad_other = swap(pick(grad_partial, 1 - core, 1), "core")
    grad_hidden = (pick(grad_partial, core, 1) + grad_other).reshape(row_total, hidden_count)
    grad_gate = grad_hidden * up_value * sigmoid_gate * (1.0 + gate_value * (1.0 - sigmoid_gate))
    grad_up = grad_hidden * silu_gate
    grad_rows = jnp.concatenate([grad_gate, grad_up], axis=1).astype(jnp.bfloat16)
    row_score = jnp.sum(grad_hidden * hidden_act.astype(jnp.float32), axis=1)

    came_second, _ = lax.optimization_barrier((came_second, row_score))
    spread = (
        kept[:quarter] + came_second.astype(jnp.float32) + came.astype(jnp.float32)
    ).astype(jnp.bfloat16)
    unit = quarter // lax.axis_size(REST)
    gathered = lax.all_to_all(
        spread.reshape(-1, unit, half), REST, split_axis=0, concat_axis=0, tiled=True
    ).reshape(-1, 2, unit, half)
    returned_score = send_back(row_score.reshape(expert_count, capacity), source)
    slot_index = lax.broadcasted_iota(jnp.int32, (expert_count, capacity), 1)
    live_rows = (slot_index < counts[:, None]).astype(jnp.float32)
    route_grad = live_rows * returned_score / route_weight.reshape(expert_count, capacity)

    total = jnp.sum(gathered.astype(jnp.float32), axis=0) / replica_count
    weight_grad = jnp.concatenate([total[0], total[1]], axis=1)[None]
    return (grad_rows, weight_grad, route_grad.reshape(row_total))


def solution(mesh):
    fine = Mesh(mesh.devices.reshape(2, 4, 2, 2, 3, 2, 2, 2), DEVICE)
    in_specs = (P(DEVICE, None), P(DEVICE), P(DEVICE), P(DEVICE, None), P(EXPERT, None, None))
    out_specs = (P(DEVICE, None), P(EXPERT, EDATA, None), P(DEVICE))
    return jax.shard_map(body, mesh=fine, in_specs=in_specs, out_specs=out_specs, check_vma=False)
```
